128 devices in a mesh: wide: 32 (over x, y, core), narrow: 4 (over z).
Axes of the slice: x: 4, y: 4, z: 4, core: 2. Of those that a mesh axis runs over, the one named last changes fastest.
Arguments:
- student_hidden: bfloat16 [512, 4096], P(('wide', 'narrow'))
- teacher_hidden: bfloat16 [512, 4096], P(('wide', 'narrow'))
- student_head: bfloat16 [4096, 147456], P(None, ('wide', 'narrow')), may hold values from -0.09375 to 0.09375
- teacher_head: bfloat16 [4096, 147456], P(None, ('wide', 'narrow')), may hold values from -0.09375 to 0.09375
- group_counts: int32 [32], replicated, may hold values from 8 to 16, as said below
- group_offsets: int32 [32], replicated, may hold values from 0 to 496, as said below
Outputs:
- token_kl: float32 [512], P(('wide', 'narrow'))
- hidden_grad: bfloat16 [512, 4096], P(('wide', 'narrow'))
The draws below stay inside these ranges and needn't reach their ends.
Inputs may be any that keep to these rules, and one draw needn't show every extreme that they name: Group g owns the 16 consecutive token slots from g * 16; its first group_counts[g] slots are live, and some group is full in every draw. The teacher row spans [group_offsets[g], group_offsets[g] + group_counts[g]) of the groups are disjoint and lie inside the 512 rows.
All inputs are finite; a program needn't handle non-finite values.
Results may differ from the reference program's by a relative error of at most 0.0047.
Values may be sent and summed in bfloat16 or wider, within the bound.
A program may use at most 128 MiB of HBM per device.

```python
import math
import jax
import jax.numpy as jnp
from jax import lax

D = 4096
V = 147456
TOK_G = 16
TOKENS = 512
NGROUPS = 32


def scaled_rows(key, base, scale_lo, scale_hi, big_share, big_scale):
    first, second = jax.random.split(key)
    logs = jax.random.uniform(first, (base.shape[0], 1), jnp.float32, jnp.log(scale_lo), jnp.log(scale_hi))
    picked = jax.random.uniform(second, (base.shape[0], 1), jnp.float32) < big_share
    scales = jnp.where(picked, big_scale, jnp.exp(logs))
    return base * scales


def hidden_rows(key):
    first, second = jax.random.split(key)
    base = jax.random.normal(first, (TOKENS, D), jnp.float32)
    rows = scaled_rows(second, base, 1.5, 6.0, 0.0, 1.0)
    return rows.astype(jnp.bfloat16)


def draw_student_hidden(key, part):
    key = jax.random.fold_in(key, 11)
    return hidden_rows(key)


def draw_teacher_hidden(key, part):
    key = jax.random.fold_in(key, 23)
    return hidden_rows(key)


def group_layout(key):
    first, second = jax.random.split(key)
    counts = jax.random.randint(first, (NGROUPS,), TOK_G // 2, TOK_G + 1)
    order = jax.random.permutation(second, NGROUPS)
    positions = jnp.arange(NGROUPS, dtype=jnp.int32)
    ordered = counts[order]
    ordered = jnp.where(positions == NGROUPS - 1, TOK_G, ordered)
    ordered = jnp.where(positions == 0, TOK_G // 2, ordered).astype(jnp.int32)
    starts = jnp.cumsum(ordered) - ordered
    starts = jnp.where(positions == NGROUPS - 1, TOKENS - TOK_G, starts).astype(jnp.int32)
    counts = jnp.zeros((NGROUPS,), jnp.int32).at[order].set(ordered)
    offsets = jnp.zeros((NGROUPS,), jnp.int32).at[order].set(starts)
    return (counts, offsets)


def draw_group_counts(key, part):
    counts, offsets = group_layout(key)
    return counts


def draw_group_offsets(key, part):
    counts, offsets = group_layout(key)
    return offsets


def block_levels(rng, dims, cuts, least, largest):
    def one(dim, parts):
        draws = jax.random.uniform(jax.random.fold_in(jax.random.fold_in(rng, 6), dim), (parts,), jnp.float32, least / len(cuts), largest / len(cuts))
        return jnp.repeat(jnp.exp(draws), dims[dim] // parts).reshape((-1,) + (1,) * (len(dims) - dim - 1))

    level = one(*cuts[0])
    for cut in cuts[1:]:
        level = level * one(*cut)
    return level


def centred(stream_key, extent, deviation, bound, cuts=(), kind=jnp.bfloat16):
    gain = block_levels(stream_key, extent, cuts, -0.22, 0.18) if cuts else 1.0
    values = jax.random.normal(stream_key, extent, jnp.float32) * deviation * gain
    return jnp.minimum(jnp.maximum(values, -bound), bound).astype(kind)


def setup_inputs(seed: int = 0) -> dict:
    arg_keys = jax.random.split(jax.random.key(seed), 7)
    return {
        "student_hidden": draw_student_hidden(jax.random.fold_in(arg_keys[6], 71), 0),
        "teacher_hidden": draw_teacher_hidden(jax.random.fold_in(arg_keys[6], 71), 0),
        "student_head": centred(arg_keys[2], (D, V), D ** -0.5, 0.09375, ((1, 128),)),
        "teacher_head": centred(arg_keys[3], (D, V), D ** -0.5, 0.09375, ((1, 128),)),
        "group_counts": draw_group_counts(jax.random.fold_in(arg_keys[6], 71), 0),
        "group_offsets": draw_group_offsets(jax.random.fold_in(arg_keys[6], 71), 0),
    }


def block_terms(student_rows, teacher_rows, live, student_head, teacher_head):
    student_logits = jnp.dot(student_rows, student_head, preferred_element_type=jnp.float32)
    teacher_logits = jnp.dot(teacher_rows, teacher_head, preferred_element_type=jnp.float32)
    smax = jnp.max(student_logits, axis=1, keepdims=True)
    tmax = jnp.max(teacher_logits, axis=1, keepdims=True)
    sexp = jnp.exp(student_logits - smax)
    texp = jnp.exp(teacher_logits - tmax)
    ssum = jnp.sum(sexp, axis=1)
    tsum = jnp.sum(texp, axis=1)
    tcross = jnp.sum(texp * (teacher_logits - student_logits), axis=1)
    value = tcross / tsum - tmax[:, 0] - jnp.log(tsum) + smax[:, 0] + jnp.log(ssum)
    token_kl = jnp.where(live, value, jnp.float32(0.0))
    diff = sexp / ssum[:, None] - texp / tsum[:, None]
    prob_diff = jnp.where(live[:, None], diff, jnp.float32(0.0)).astype(jnp.bfloat16)
    grad = lax.dot_general(prob_diff, student_head, (((1,), (1,)), ((), ())), preferred_element_type=jnp.float32)
    return token_kl, grad.astype(jnp.bfloat16)


def reference(student_hidden, teacher_hidden, student_head, teacher_head, group_counts, group_offsets):
    slots = jnp.arange(TOKENS, dtype=jnp.int32)
    group = slots // TOK_G
    within = slots % TOK_G
    live = within < group_counts[group]
    pair = jnp.minimum(group_offsets[group] + within, TOKENS - 1).astype(jnp.int32)
    paired = teacher_hidden[pair]
    block = math.gcd(TOKENS, 64)
    count = TOKENS // block

    def one_block(items):
        rows, teach, alive = items
        return block_terms(rows, teach, alive, student_head, teacher_head)

    kl_blocks, grad_blocks = lax.map(one_block, (student_hidden.reshape(count, block, D), paired.reshape(count, block, D), live.reshape(count, block)))
    return kl_blocks.reshape(TOKENS), grad_blocks.reshape(TOKENS, D)
```

```python
import jax
import jax.numpy as jnp
from jax import lax
from jax.experimental import pallas as pl
from jax.experimental.pallas import tpu as pltpu
from jax.sharding import PartitionSpec as P

MESH = pl.DeviceIdType.MESH
F32, BF16 = jnp.float32, jnp.bfloat16
AXES = ("z", "x", "y")
GATHER = ((0, 384, ("x", "y", "z")), (384, 384, ("y", "z", "x")), (768, 256, ("z", "x", "y")))
ORDERS = (("z", "x", "y"), ("x", "y", "z"), ("y", "z", "x"))
CHUNKS = 8
COPIES = 264
VOCAB = 1152
TILES = VOCAB // 128


def kernel(
    student_ref, teacher_ref, shead_hbm, thead_hbm, count_ref, offset_ref,
    kl_ref, grad_ref,
    shead, thead, xs, xt, sl, tl, et, pd,
    pre_send, pre_recv, block, stat, st_send, st_recv,
    core_send, core_recv, own, stage0, recv0, mid0, cur1, stage1, recv1, mid1, cur2, recv2, cur3, fin_send, fin_recv,
    send_sem, recv_sem, load_sem,
):
    wide = lax.axis_index("wide")
    me = {"z": lax.axis_index("narrow"), "x": wide // 8, "y": lax.rem(wide // 2, 4)}
    core = lax.rem(wide, 2)

    def device(at, c):
        return ((at["x"] * 4 + at["y"]) * 2 + c, at["z"])

    def shifted(axis, delta):
        return {**me, axis: lax.rem(me[axis] + delta, 4)}

    def peer(axis, delta):
        return device(shifted(axis, delta), core)

    sibling = device(me, 1 - core)
    started = []

    def send(src, dst, to):
        index = len(started)
        copy = pltpu.make_async_remote_copy(
            src_ref=src, dst_ref=dst, send_sem=send_sem.at[index], recv_sem=recv_sem.at[index],
            device_id=to, device_id_type=MESH,
        )
        copy.start()
        started.append(copy)
        return copy

    loads = [
        pltpu.make_async_copy(thead_hbm, thead, load_sem.at[0]),
        pltpu.make_async_copy(shead_hbm, shead, load_sem.at[1]),
    ]
    for load in loads:
        load.start()

    barrier = pltpu.get_barrier_semaphore()
    friends = [peer(axis, delta) for axis in AXES for delta in (1, 2, 3)] + [sibling]
    for friend in friends:
        pl.semaphore_signal(barrier, inc=1, device_id=friend, device_id_type=MESH)

    for q in range(4):
        pre_send[q, 0:4, :] = teacher_ref[:, q * 1024:(q + 1) * 1024].astype(F32)
        pre_send[q, 4:8, :] = student_ref[:, q * 1024:(q + 1) * 1024].astype(F32)
    pl.semaphore_wait(barrier, len(friends))

    z = me["z"]
    first = []
    for delta in (1, 2, 3):
        to = shifted("z", delta)
        first.append(send(pre_send.at[to["z"]], pre_recv.at[z], device(to, core)))
    pre_recv[z] = pre_send[z]
    for copy in first:
        copy.wait_recv()
    for row, rows in ((0, xt), (4, xs)):
        for s in range(4):
            block[4 * s:4 * s + 4, :] = pre_recv[s, row:row + 4, :]
        rows[z, me["x"], me["y"], core] = block[...].astype(BF16)

    def region(rows, part, free, at, c, half=None):
        start, width, order = GATHER[part]
        index = []
        for axis in AXES:
            if axis not in free:
                index.append(at[axis])
            elif half is not None and axis == order[0]:
                index.append(pl.ds(2 * half, 2))
            else:
                index.append(pl.ds(0, 4))
        return rows.at[(*index, c, pl.ds(0, 16), pl.ds(start, width))]

    parts = range(len(GATHER))

    def to_core(rows, part, free, at):
        here = region(rows, part, free, at, core)
        return send(here, here, sibling)

    def phase0(rows):
        copies = []
        for part in parts:
            axis = GATHER[part][2][0]
            here = region(rows, part, (), me, core)
            copies.append([send(here, here, peer(axis, delta)) for delta in (1, 3, 2)])
        return copies

    def start_phase(rows, step):
        copies = []
        for part in parts:
            order = GATHER[part][2]
            axis, free = order[step], order[:step]
            halves = [region(rows, part, free, me, core, half) for half in (0, 1)]
            group = {}
            group["l0"] = send(halves[0], halves[0], peer(axis, 1))
            group["r1"] = send(halves[1], halves[1], peer(axis, 3))
            group["l1"] = send(halves[1], halves[1], peer(axis, 1))
            group["r0"] = send(halves[0], halves[0], peer(axis, 3))
            copies.append(group)
        return copies

    def pass_on(rows, step, copies):
        for part in parts:
            order = GATHER[part][2]
            axis, free = order[step], order[:step]
            group = copies[part]
            group["l0"].wait_recv()
            here = region(rows, part, free, shifted(axis, 3), core, 0)
            group["lf"] = send(here, here, peer(axis, 1))
            group["r1"].wait_recv()
            here = region(rows, part, free, shifted(axis, 1), core, 1)
            group["rf"] = send(here, here, peer(axis, 3))

    def finish(copies, names):
        for group in copies:
            for name in names:
                group[name].wait_recv()

    def own_to_core(rows):
        return [to_core(rows, part, GATHER[part][2][:2], me) for part in parts]

    def near_to_core(rows, copies):
        finish(copies, ("l1", "r0"))
        return [
            to_core(rows, part, GATHER[part][2][:2], shifted(GATHER[part][2][2], delta))
            for part in parts for delta in (3, 1)
        ]

    def far_to_core(rows, copies):
        finish(copies, ("lf", "rf"))
        return [
            to_core(rows, part, GATHER[part][2][:2], shifted(GATHER[part][2][2], 2)) for part in parts
        ]

    t0 = phase0(xt)
    s0 = phase0(xs)
    for group in t0:
        for copy in group:
            copy.wait_recv()
    t1 = start_phase(xt, 1)
    for group in s0:
        for copy in group:
            copy.wait_recv()
    s1 = start_phase(xs, 1)
    pass_on(xt, 1, t1)
    pass_on(xs, 1, s1)
    finish(t1, ("l1", "r0", "lf", "rf"))
    t2 = start_phase(xt, 2)
    tcore = own_to_core(xt)
    finish(s1, ("l1", "r0", "lf", "rf"))
    pass_on(xt, 2, t2)
    s2 = start_phase(xs, 2)
    score = own_to_core(xs)
    tcore += near_to_core(xt, t2)
    tcore += far_to_core(xt, t2)
    for copy in tcore:
        copy.wait_recv()
    loads[0].wait()

    def logits(rows, head, out, tile, count):
        total = None
        for q in range(4):
            part = jnp.dot(
                rows[q].reshape(512, 1024),
                head[q * 1024:(q + 1) * 1024, tile * 128:(tile + count) * 128],
                preferred_element_type=F32,
            )
            total = part if total is None else total + part
        for i in range(count):
            out[tile + i] = total[:, i * 128:(i + 1) * 128]

    logits(xt, thead, tl, 0, 2)
    logits(xt, thead, tl, 2, 2)
    pass_on(xs, 2, s2)
    logits(xt, thead, tl, 4, 2)
    score += near_to_core(xs, s2)
    logits(xt, thead, tl, 6, 2)
    score += far_to_core(xs, s2)
    logits(xt, thead, tl, 8, 1)
    for copy in score:
        copy.wait_recv()
    loads[1].wait()
    for tile in (0, 2, 4, 6):
        logits(xs, shead, sl, tile, 2)
    logits(xs, shead, sl, 8, 1)

    lane = lax.broadcasted_iota(jnp.int32, (16, 128), 1)

    def terms(g, carry):
        at = pl.ds(pl.multiple_of(g * 16, 16), 16)
        pair = pl.ds(offset_ref[g], 16)
        s = [sl[j, at, :] for j in range(TILES)]
        t = [tl[j, pair, :] for j in range(TILES)]
        smax, tmax = s[0], t[0]
        for j in range(1, TILES):
            smax = jnp.maximum(smax, s[j])
            tmax = jnp.maximum(tmax, t[j])
        smax = jnp.max(smax, axis=1, keepdims=True)
        tmax = jnp.max(tmax, axis=1, keepdims=True)
        ssum = tsum = cross = jnp.zeros((16, 128), F32)
        for j in range(TILES):
            e = jnp.exp(s[j] - smax)
            sl[j, at, :] = e
            ssum = ssum + e
            e = jnp.exp(t[j] - tmax)
            et[j, at, :] = e
            tsum = tsum + e
            cross = cross + e * (t[j] - s[j])
        ssum = jnp.sum(ssum, axis=1, keepdims=True)
        tsum = jnp.sum(tsum, axis=1, keepdims=True)
        cross = jnp.sum(cross, axis=1, keepdims=True)
        tile = jnp.where(lane == 0, smax, jnp.where(lane == 1, tmax, jnp.where(lane == 2, ssum, jnp.where(lane == 3, tsum, cross))))
        stat[at, :] = tile
        return carry

    lax.fori_loop(0, 32, terms, 0, unroll=2)

    local = stat[...].T[0:8, :]
    now = local
    slot = 0
    for level, axis in enumerate(("core", "x", "y", "z")):
        st_send[level] = now
        if axis == "core":
            copies = [send(st_send.at[level], st_recv.at[slot], sibling)]
        else:
            copies = [
                send(st_send.at[level], st_recv.at[slot + i], peer(axis, delta))
                for i, delta in enumerate((1, 3, 2))
            ]
        for copy in copies:
            copy.wait_recv()
        members = [now] + [st_recv[slot + i] for i in range(len(copies))]
        slot += len(copies)
        smax, tmax = members[0][0:1], members[0][1:2]
        for member in members[1:]:
            smax = jnp.maximum(smax, member[0:1])
            tmax = jnp.maximum(tmax, member[1:2])
        ssum = tsum = cross = jnp.zeros((1, 512), F32)
        for member in members:
            a = jnp.exp(member[0:1] - smax)
            b = jnp.exp(member[1:2] - tmax)
            ssum = ssum + member[2:3] * a
            tsum = tsum + member[3:4] * b
            cross = cross + member[4:5] * b
        now = jnp.concatenate([smax, tmax, ssum, tsum, cross, cross, cross, cross], axis=0)
    value = cross / tsum - tmax - jnp.log(tsum) + smax + jnp.log(ssum)
    sscale = jnp.exp(local[0:1] - smax) / ssum
    tscale = jnp.exp(local[1:2] - tmax) / tsum
    filler = jnp.zeros((125, 512), F32)
    stat[...] = jnp.concatenate([sscale, tscale, value, filler], axis=0).T

    row = lax.broadcasted_iota(jnp.int32, (16, 128), 0)
    mine = stat[pl.ds(pl.multiple_of(wide * 16, 16), 16), :]
    mine = jnp.where(row < count_ref[wide], mine, 0.0)
    for i in range(4):
        kl_ref[i] = jnp.sum(jnp.where((row == z * 4 + i) & (lane == 2), mine, 0.0))

    def prob_diff(pair, carry):
        for c in range(2):
            g = pair * 2 + c
            half = core if c else 1 - core
            at = pl.ds(pl.multiple_of(g * 16, 16), 16)
            scale = stat[at, :]
            live = row < count_ref[g]
            a = jnp.where(live, jnp.broadcast_to(scale[:, 0:1], (16, 128)), 0.0)
            b = jnp.where(live, jnp.broadcast_to(scale[:, 1:2], (16, 128)), 0.0)
            for j in range(TILES):
                pd[half, pair, :, j * 128:(j + 1) * 128] = (sl[j, at, :] * a - et[j, at, :] * b).astype(BF16)
        return carry

    lax.fori_loop(0, 16, prob_diff, 0)

    def grad_matmul(j):
        weights = jnp.concatenate([shead[q * 1024 + j * 128:q * 1024 + (j + 1) * 128, :] for q in range(4)], axis=0)
        out = lax.dot_general(
            pd[...].reshape(512, VOCAB), weights, (((1,), (1,)), ((), ())), preferred_element_type=F32
        )
        for q in range(4):
            piece = out[:, q * 128:(q + 1) * 128]
            core_send[j, q] = piece[0:256].astype(BF16).reshape(4, 4, 16, 128)
            own[j, q] = piece[256:512].reshape(4, 4, 16, 128)
        return send(core_send.at[j], core_recv.at[j], sibling)

    def pick(ref, j, axis, axes, q):
        index = [slice(None)] * len(axes)
        index[axes.index(axis)] = q
        return ref[(j, *index)]

    def scatter_start(j, cur, axis, axes, stage, recv, mid):
        right, left = peer(axis, 1), peer(axis, 3)
        stage[j, 2] = pick(cur, j, axis, axes, lax.rem(me[axis] + 2, 4)).astype(BF16)
        copies = {}
        copies["lm"] = send(stage.at[j, 2, pl.ds(0, 2)], mid.at[j, 0], right)
        copies["rm"] = send(stage.at[j, 2, pl.ds(2, 2)], mid.at[j, 1], left)
        stage[j, 0, 2:4] = pick(cur, j, axis, axes, lax.rem(me[axis] + 1, 4))[2:4].astype(BF16)
        stage[j, 1, 0:2] = pick(cur, j, axis, axes, lax.rem(me[axis] + 3, 4))[0:2].astype(BF16)
        copies["l1"] = send(stage.at[j, 0, pl.ds(2, 2)], recv.at[j, 0, pl.ds(2, 2)], right)
        copies["r0"] = send(stage.at[j, 1, pl.ds(0, 2)], recv.at[j, 1, pl.ds(0, 2)], left)
        return copies

    def scatter_pass(j, cur, axis, axes, stage, recv, mid, copies):
        right, left = peer(axis, 1), peer(axis, 3)
        copies["lm"].wait_recv()
        ours = pick(cur, j, axis, axes, lax.rem(me[axis] + 1, 4))[0:2]
        stage[j, 0, 0:2] = (ours + mid[j, 0].astype(F32)).astype(BF16)
        copies["l0"] = send(stage.at[j, 0, pl.ds(0, 2)], recv.at[j, 0, pl.ds(0, 2)], right)
        copies["rm"].wait_recv()
        ours = pick(cur, j, axis, axes, lax.rem(me[axis] + 3, 4))[2:4]
        stage[j, 1, 2:4] = (ours + mid[j, 1].astype(F32)).astype(BF16)
        copies["r1"] = send(stage.at[j, 1, pl.ds(2, 2)], recv.at[j, 1, pl.ds(2, 2)], left)

    def scatter_end(j, cur, axis, axes, recv, copies):
        for name in ("l1", "r0", "l0", "r1"):
            copies[name].wait_recv()
        return pick(cur, j, axis, axes, me[axis]) + recv[j, 0].astype(F32) + recv[j, 1].astype(F32)

    state = [{} for _ in range(CHUNKS)]

    def axes_of(j):
        order = ORDERS[j % 3]
        after = tuple(axis for axis in AXES if axis != order[0])
        return order, after

    def step(j, level):
        order, after = axes_of(j)
        mem = state[j]
        if level == 0:
            mem["core"] = grad_matmul(j)
        elif level == 1:
            mem["core"].wait_recv()
            own[j] = own[j] + core_recv[j].astype(F32)
            mem["a"] = scatter_start(j, own, order[0], AXES, stage0, recv0, mid0)
        elif level == 2:
            scatter_pass(j, own, order[0], AXES, stage0, recv0, mid0, mem["a"])
        elif level == 3:
            cur1[j] = scatter_end(j, own, order[0], AXES, recv0, mem["a"])
            mem["b"] = scatter_start(j, cur1, order[1], after, stage1, recv1, mid1)
        elif level == 4:
            scatter_pass(j, cur1, order[1], after, stage1, recv1, mid1, mem["b"])
        elif level == 5:
            cur2[j] = scatter_end(j, cur1, order[1], after, recv1, mem["b"])
            mem["c"] = [
                send(cur2.at[j, shifted(order[2], delta)[order[2]]], recv2.at[j, i], peer(order[2], delta))
                for i, delta in enumerate((1, 3, 2))
            ]
        else:
            for copy in mem["c"]:
                copy.wait_recv()
            cur3[:, j * 128:(j + 1) * 128] = cur2[j, me[order[2]]] + recv2[j, 0] + recv2[j, 1] + recv2[j, 2]

    for time in range(CHUNKS + 6):
        for level in range(6, -1, -1):
            if 0 <= time - level < CHUNKS:
                step(time - level, level)

    for q in range(4):
        fin_send[q] = cur3[4 * q:4 * q + 4, :]
    last = []
    for delta in (1, 2, 3):
        to = shifted("z", delta)
        last.append(send(fin_send.at[to["z"]], fin_recv.at[z], device(to, core)))
    fin_recv[z] = fin_send[z]
    for copy in last:
        copy.wait_recv()
    for q in range(4):
        grad_ref[:, q * 1024:(q + 1) * 1024] = fin_recv[q].astype(BF16)
    for copy in started:
        copy.wait_send()


def shards(student_hidden, teacher_hidden, student_head, teacher_head, group_counts, group_offsets):
    vmem = pl.BlockSpec(memory_space=pltpu.VMEM)
    smem = pl.BlockSpec(memory_space=pltpu.SMEM)
    hbm = pl.BlockSpec(memory_space=pl.ANY)
    rows = pltpu.VMEM((4, 4, 4, 2, 16, 1024), BF16)
    head = pltpu.VMEM((4096, VOCAB), BF16)
    table = pltpu.VMEM((TILES, 512, 128), F32)
    scratch = [
        head, head, rows, rows, table, table, table,
        pltpu.VMEM((2, 16, 16, VOCAB), BF16),
        pltpu.VMEM((4, 8, 1024), F32),
        pltpu.VMEM((4, 8, 1024), F32),
        pltpu.VMEM((16, 1024), F32),
        pltpu.VMEM((512, 128), F32),
        pltpu.VMEM((4, 8, 512), F32),
        pltpu.VMEM((10, 8, 512), F32),
        pltpu.VMEM((CHUNKS, 4, 4, 4, 16, 128), BF16),
        pltpu.VMEM((CHUNKS, 4, 4, 4, 16, 128), BF16),
        pltpu.VMEM((CHUNKS, 4, 4, 4, 16, 128), F32),
        pltpu.VMEM((CHUNKS, 3, 4, 4, 16, 128), BF16),
        pltpu.VMEM((CHUNKS, 2, 4, 4, 16, 128), BF16),
        pltpu.VMEM((CHUNKS, 2, 2, 4, 16, 128), BF16),
        pltpu.VMEM((CHUNKS, 4, 4, 16, 128), F32),
        pltpu.VMEM((CHUNKS, 3, 4, 16, 128), BF16),
        pltpu.VMEM((CHUNKS, 2, 4, 16, 128), BF16),
        pltpu.VMEM((CHUNKS, 2, 2, 16, 128), BF16),
        pltpu.VMEM((CHUNKS, 4, 16, 128), F32),
        pltpu.VMEM((CHUNKS, 3, 16, 128), F32),
        pltpu.VMEM((16, 1024), F32),
        pltpu.VMEM((4, 4, 1024), F32),
        pltpu.VMEM((4, 4, 1024), F32),
        pltpu.SemaphoreType.DMA((COPIES,)),
        pltpu.SemaphoreType.DMA((COPIES,)),
        pltpu.SemaphoreType.DMA((2,)),
    ]
    return pl.pallas_call(
        kernel,
        out_shape=(
            jax.ShapeDtypeStruct((4,), F32),
            jax.ShapeDtypeStruct((4, 4096), BF16),
        ),
        in_specs=[vmem, vmem, hbm, hbm, smem, smem],
        out_specs=(smem, vmem),
        scratch_shapes=scratch,
        compiler_params=pltpu.CompilerParams(
            collective_id=0, has_side_effects=True, vmem_limit_bytes=60 << 20
        ),
        cost_estimate=pl.CostEstimate(flops=14495514624, bytes_accessed=19000000, transcendentals=1200000),
    )(student_hidden, teacher_hidden, student_head, teacher_head, group_counts, group_offsets)


def solution(mesh):
    both = ("wide", "narrow")
    return jax.shard_map(
        shards,
        mesh=mesh,
        in_specs=(P(both, None), P(both, None), P(None, both), P(None, both), P(), P()),
        out_specs=(P(both), P(both, None)),
        check_vma=False,
    )
```

```python
import jax
import jax.numpy as jnp
from jax import lax
from jax.experimental import pallas as pl
from jax.experimental.pallas import tpu as pltpu
from jax.sharding import PartitionSpec as P

MESH = pl.DeviceIdType.MESH
F32, BF16 = jnp.float32, jnp.bfloat16
AXES = ("z", "x", "y")
GATHER = ((0, 384, ("x", "y", "z")), (384, 384, ("y", "z", "x")), (768, 256, ("z", "x", "y")))
FIRST = ("z", "z", "x", "x", "x", "y", "y", "y")
THEN = {"z": "x", "x": "y", "y": "x"}
SEQUENCE = (0, 2, 5, 1, 3, 6, 4, 7)
CHUNKS = len(FIRST)
COPIES = 208
FAR_FIRST = (2, 1, 3)
VOCAB = 1152
TILES = VOCAB // 128


def kernel(
    student_hbm, teacher_hbm, shead_hbm, thead_hbm, count_hbm, offset_hbm,
    out_ref,
    student_ref, teacher_ref, count_ref, offset_ref,
    shead, thead, rows, sl, tl, et, pd,
    pre_send, pre_recv, block, stat, st_send, st_recv,
    core_send, core_recv, own, stage0, recv0,
    curz, curx, cury, stagez, stagex, stagey, recvz, recvx, recvy, curz2, recvz2,
    finz, finx, finy, gotz, gotx, goty,
    send_sem, recv_sem, load_sem,
):
    wide = lax.axis_index("wide")
    me = {"z": lax.axis_index("narrow"), "x": wide // 8, "y": lax.rem(wide // 2, 4)}
    core = lax.rem(wide, 2)

    def device(at, c):
        return ((at["x"] * 4 + at["y"]) * 2 + c, at["z"])

    def shifted(axis, delta):
        return {**me, axis: lax.rem(me[axis] + delta, 4)}

    def peer(axis, delta):
        return device(shifted(axis, delta), core)

    sibling = device(me, 1 - core)
    started = []

    def send(src, dst, to):
        index = len(started)
        copy = pltpu.make_async_remote_copy(
            src_ref=src, dst_ref=dst, send_sem=send_sem.at[index], recv_sem=recv_sem.at[index],
            device_id=to, device_id_type=MESH,
        )
        copy.start()
        started.append(copy)
        return copy

    loads = [
        pltpu.make_async_copy(src, dst, load_sem.at[i])
        for i, (src, dst) in enumerate((
            (teacher_hbm, teacher_ref), (student_hbm, student_ref), (count_hbm, count_ref),
            (offset_hbm, offset_ref), (thead_hbm, thead), (shead_hbm, shead),
        ))
    ]
    for load in loads:
        load.start()

    barrier = pltpu.get_barrier_semaphore()
    friends = [peer(axis, delta) for axis in AXES for delta in (1, 2, 3)] + [sibling]
    for friend in friends:
        pl.semaphore_signal(barrier, inc=1, device_id=friend, device_id_type=MESH)

    for load in loads[:2]:
        load.wait()
    for q in range(4):
        pre_send[q, 0:4, :] = teacher_ref[:, q * 1024:(q + 1) * 1024].astype(F32)
        pre_send[q, 4:8, :] = student_ref[:, q * 1024:(q + 1) * 1024].astype(F32)
    pl.semaphore_wait(barrier, len(friends))

    z = me["z"]
    first = []
    for delta in (1, 2, 3):
        to = shifted("z", delta)
        first.append(send(pre_send.at[to["z"]], pre_recv.at[z], device(to, core)))
    pre_recv[z] = pre_send[z]
    for copy in first:
        copy.wait_recv()
    for which in range(2):
        for s in range(4):
            block[4 * s:4 * s + 4, :] = pre_recv[s, 4 * which:4 * which + 4, :]
        rows[which, z, me["x"], me["y"], core] = block[...].astype(BF16)

    def region(part, free, at, c, which=None, half=None):
        start, width, order = GATHER[part]
        index = [pl.ds(0, 2) if which is None else which]
        for axis in AXES:
            if axis not in free:
                index.append(at[axis])
            elif half is not None and axis == order[0]:
                index.append(pl.ds(2 * half, 2))
            else:
                index.append(pl.ds(0, 4))
        return rows.at[(*index, c, pl.ds(0, 16), pl.ds(start, width))]

    parts = range(len(GATHER))

    def spread(part, step):
        order = GATHER[part][2]
        here = region(part, order[:step], me, core)
        return [send(here, here, peer(order[step], delta)) for delta in FAR_FIRST]

    def to_core(part, at, which=None):
        here = region(part, GATHER[part][2][:2], at, core, which)
        return send(here, here, sibling)

    def start_last(which, names):
        for part in parts:
            order = GATHER[part][2]
            for name in names:
                here = region(part, order[:2], me, core, which, int(name[1]))
                last[which][part][name] = send(here, here, peer(order[2], 1 if name[0] == "l" else 3))

    def pass_on(which):
        for part in parts:
            order = GATHER[part][2]
            for name, delta, half, to in (("l0", 3, 0, 1), ("r1", 1, 1, 3)):
                last[which][part][name].wait_recv()
                here = region(part, order[:2], shifted(order[2], delta), core, which, half)
                last[which][part]["far" + name] = send(here, here, peer(order[2], to))

    def near_to_core(which):
        copies = []
        for part in parts:
            for name, delta in (("l1", 3), ("r0", 1)):
                last[which][part][name].wait_recv()
                copies.append(to_core(part, shifted(GATHER[part][2][2], delta), which))
        return copies

    def far_to_core(which):
        copies = []
        for part in parts:
            for name in ("farl0", "farr1"):
                last[which][part][name].wait_recv()
            copies.append(to_core(part, shifted(GATHER[part][2][2], 2), which))
        return copies

    last = [[{} for _ in parts] for _ in range(2)]
    step0 = [spread(part, 0) for part in parts]
    step1 = []
    for part in parts:
        for copy in step0[part]:
            copy.wait_recv()
        step1.append(spread(part, 1))
    for part in parts:
        for copy in step1[part]:
            copy.wait_recv()
    start_last(0, ("l0", "r1", "l1", "r0"))
    start_last(1, ("l0", "r1"))
    cores = [[to_core(part, me) for part in parts], []]
    pass_on(0)
    start_last(1, ("l1", "r0"))
    cores[0] += near_to_core(0)
    cores[0] += far_to_core(0)
    for copy in cores[0]:
        copy.wait_recv()
    loads[4].wait()

    def logits(which, head, out, tile):
        count = min(2, TILES - tile)
        total = None
        for q in range(4):
            part = jnp.dot(
                rows[which, q].reshape(512, 1024),
                head[q * 1024:(q + 1) * 1024, tile * 128:(tile + count) * 128],
                preferred_element_type=F32,
            )
            total = part if total is None else total + part
        for i in range(count):
            out[tile + i] = total[:, i * 128:(i + 1) * 128]

    logits(0, thead, tl, 0)
    pass_on(1)
    logits(0, thead, tl, 2)
    logits(0, thead, tl, 4)
    cores[1] += near_to_core(1)
    logits(0, thead, tl, 6)
    cores[1] += far_to_core(1)
    logits(0, thead, tl, 8)
    for copy in cores[1]:
        copy.wait_recv()
    for load in (loads[2], loads[3], loads[5]):
        load.wait()
    for tile in range(0, TILES, 2):
        logits(1, shead, sl, tile)

    lane = lax.broadcasted_iota(jnp.int32, (16, 128), 1)

    def terms(g, carry):
        at = pl.ds(pl.multiple_of(g * 16, 16), 16)
        pair = pl.ds(offset_ref[g], 16)
        s = [sl[j, at, :] for j in range(TILES)]
        t = [tl[j, pair, :] for j in range(TILES)]
        smax, tmax = s[0], t[0]
        for j in range(1, TILES):
            smax = jnp.maximum(smax, s[j])
            tmax = jnp.maximum(tmax, t[j])
        smax = jnp.max(smax, axis=1, keepdims=True)
        tmax = jnp.max(tmax, axis=1, keepdims=True)
        ssum = tsum = cross = jnp.zeros((16, 128), F32)
        for j in range(TILES):
            e = jnp.exp(s[j] - smax)
            sl[j, at, :] = e
            ssum = ssum + e
            e = jnp.exp(t[j] - tmax)
            et[j, at, :] = e
            tsum = tsum + e
            cross = cross + e * (t[j] - s[j])
        ssum = jnp.sum(ssum, axis=1, keepdims=True)
        tsum = jnp.sum(tsum, axis=1, keepdims=True)
        cross = jnp.sum(cross, axis=1, keepdims=True)
        tile = jnp.where(lane == 0, smax, jnp.where(lane == 1, tmax, jnp.where(lane == 2, ssum, jnp.where(lane == 3, tsum, cross))))
        stat[at, :] = tile
        return carry

    lax.fori_loop(0, 32, terms, 0, unroll=4)

    local = stat[...].T[0:8, :]
    now = local
    slot = 0
    for level, axis in enumerate(("core", "x", "y", "z")):
        st_send[level] = now
        if axis == "core":
            copies = [send(st_send.at[level], st_recv.at[slot], sibling)]
        else:
            copies = [
                send(st_send.at[level], st_recv.at[slot + i], peer(axis, delta))
                for i, delta in enumerate(FAR_FIRST)
            ]
        for copy in copies:
            copy.wait_recv()
        members = [now] + [st_recv[slot + i] for i in range(len(copies))]
        slot += len(copies)
        smax, tmax = members[0][0:1], members[0][1:2]
        for member in members[1:]:
            smax = jnp.maximum(smax, member[0:1])
            tmax = jnp.maximum(tmax, member[1:2])
        ssum = tsum = cross = jnp.zeros((1, 512), F32)
        for member in members:
            a = jnp.exp(member[0:1] - smax)
            b = jnp.exp(member[1:2] - tmax)
            ssum = ssum + member[2:3] * a
            tsum = tsum + member[3:4] * b
            cross = cross + member[4:5] * b
        now = jnp.concatenate([smax, tmax, ssum, tsum, cross, cross, cross, cross], axis=0)
    value = cross / tsum - tmax - jnp.log(tsum) + smax + jnp.log(ssum)
    sscale = jnp.exp(local[0:1] - smax) / ssum
    tscale = jnp.exp(local[1:2] - tmax) / tsum
    filler = jnp.zeros((125, 512), F32)
    stat[...] = jnp.concatenate([sscale, tscale, value, filler], axis=0).T

    row = lax.broadcasted_iota(jnp.int32, (16, 128), 0)
    four = lax.broadcasted_iota(jnp.int32, (4, 128), 0)
    mine = stat[pl.ds(wide * 16 + z * 4, 4), :]
    mine = jnp.where(four + z * 4 < count_ref[wide], jnp.broadcast_to(mine[:, 2:3], (4, 128)), 0.0)
    out_ref[:, 4096:4224] = mine

    def prob_diff(pair, carry):
        for c in range(2):
            g = pair * 2 + c
            half = core if c else 1 - core
            at = pl.ds(pl.multiple_of(g * 16, 16), 16)
            scale = stat[at, :]
            live = row < count_ref[g]
            a = jnp.where(live, jnp.broadcast_to(scale[:, 0:1], (16, 128)), 0.0)
            b = jnp.where(live, jnp.broadcast_to(scale[:, 1:2], (16, 128)), 0.0)
            for j in range(TILES):
                pd[half, pair, :, j * 128:(j + 1) * 128] = (sl[j, at, :] * a - et[j, at, :] * b).astype(BF16)
        return carry

    lax.fori_loop(0, 16, prob_diff, 0)

    def grad_matmul(j):
        weights = jnp.concatenate([shead[q * 1024 + j * 128:q * 1024 + (j + 1) * 128, :] for q in range(4)], axis=0)
        out = lax.dot_general(
            pd[...].reshape(512, VOCAB), weights, (((1,), (1,)), ((), ())), preferred_element_type=F32
        )
        for q in range(4):
            piece = out[:, q * 128:(q + 1) * 128]
            core_send[j, q] = piece[0:256].astype(BF16).reshape(4, 4, 16, 128)
            own[j, q] = piece[256:512].reshape(4, 4, 16, 128)
        return send(core_send.at[j], core_recv.at[j], sibling)

    def pick(ref, j, axis, q):
        index = [slice(None)] * 3
        index[AXES.index(axis)] = q
        return ref[(j, *index)]

    boxes = {}

    def first_start(j, core_copy):
        axis = FIRST[j]
        core_copy.wait_recv()
        boxes[j] = []
        for i, delta in enumerate(FAR_FIRST):
            q = shifted(axis, delta)[axis]
            stage0[j, i] = (pick(own, j, axis, q) + pick(core_recv, j, axis, q).astype(F32)).astype(BF16)
            boxes[j].append(send(stage0.at[j, i], recv0.at[j, i], peer(axis, delta)))

    cur = {"z": curz, "x": curx, "y": cury}
    stage = {"z": stagez, "x": stagex, "y": stagey}
    recv = {"z": recvz, "x": recvx, "y": recvy}

    def first_end(j):
        axis = FIRST[j]
        for copy in boxes[j]:
            copy.wait_recv()
        total = pick(own, j, axis, me[axis]) + pick(core_recv, j, axis, me[axis]).astype(F32)
        for i in range(3):
            total = total + recv0[j, i].astype(F32)
        place = j - FIRST.index(axis)
        for q in range(4):
            cur[axis][q, place] = total[q] if axis == "z" else total[:, q]

    def second_start(axis):
        copies = []
        for i, delta in enumerate(FAR_FIRST):
            q = shifted(THEN[axis], delta)[THEN[axis]]
            stage[axis][i] = cur[axis][q].astype(BF16)
            copies.append(send(stage[axis].at[i], recv[axis].at[i], peer(THEN[axis], delta)))
        return copies

    def second_end(axis, copies):
        for copy in copies:
            copy.wait_recv()
        total = cur[axis][me[THEN[axis]]]
        for i in range(3):
            total = total + recv[axis][i].astype(F32)
        return total

    def rows_start(total, fin, got):
        for q in range(4):
            fin[q] = total[:, :, 4 * q:4 * q + 4, :]
        copies = []
        for delta in FAR_FIRST:
            q = shifted("z", delta)["z"]
            copies.append(send(fin.at[q], got.at[z], peer("z", delta)))
        got[z] = fin[z]
        return copies

    waiting = []
    for n, j in enumerate(SEQUENCE):
        waiting.append((j, grad_matmul(j)))
        if n >= 1:
            first_start(*waiting.pop(0))
    first_start(*waiting.pop(0))

    for j in (0, 1):
        first_end(j)
    zcopies = second_start("z")
    for j in (2, 3, 4):
        first_end(j)
    xcopies = second_start("x")
    for j in (5, 6, 7):
        first_end(j)
    ycopies = second_start("y")
    total = second_end("z", zcopies)
    for q in range(4):
        curz2[q] = total[:, q]
    zcopies = [
        send(curz2.at[shifted("y", delta)["y"]], recvz2.at[i], peer("y", delta))
        for i, delta in enumerate(FAR_FIRST)
    ]
    xcopies = rows_start(second_end("x", xcopies), finx, gotx)
    ycopies = rows_start(second_end("y", ycopies), finy, goty)
    for copy in zcopies:
        copy.wait_recv()
    total = curz2[me["y"]] + recvz2[0] + recvz2[1] + recvz2[2]
    zcopies = rows_start(total[None], finz, gotz)
    for axis, copies, got in (("x", xcopies, gotx), ("y", ycopies, goty)):
        for copy in copies:
            copy.wait_recv()
        total = got[0] + got[1] + got[2] + got[3]
        for place in range(3):
            for q in range(4):
                at = q * 1024 + (FIRST.index(axis) + place) * 128
                out_ref[:, at:at + 128] = total[place, q]
    for copy in zcopies:
        copy.wait_recv()
    for place in range(2):
        for q in range(4):
            at = q * 1024 + place * 128
            out_ref[:, at:at + 128] = gotz[q, 0, place]
    for copy in started:
        copy.wait_send()


def shards(student_hidden, teacher_hidden, student_head, teacher_head, group_counts, group_offsets):
    hbm = pl.BlockSpec(memory_space=pl.ANY)
    head = pltpu.VMEM((4096, VOCAB), BF16)
    table = pltpu.VMEM((TILES, 512, 128), F32)
    scratch = [
        pltpu.VMEM((4, 4096), BF16),
        pltpu.VMEM((4, 4096), BF16),
        pltpu.SMEM((32,), jnp.int32),
        pltpu.SMEM((32,), jnp.int32),
        head, head,
        pltpu.VMEM((2, 4, 4, 4, 2, 16, 1024), BF16),
        table, table, table,
        pltpu.VMEM((2, 16, 16, VOCAB), BF16),
        pltpu.VMEM((4, 8, 1024), F32),
        pltpu.VMEM((4, 8, 1024), F32),
        pltpu.VMEM((16, 1024), F32),
        pltpu.VMEM((512, 128), F32),
        pltpu.VMEM((4, 8, 512), F32),
        pltpu.VMEM((10, 8, 512), F32),
        pltpu.VMEM((CHUNKS, 4, 4, 4, 16, 128), BF16),
        pltpu.VMEM((CHUNKS, 4, 4, 4, 16, 128), BF16),
        pltpu.VMEM((CHUNKS, 4, 4, 4, 16, 128), F32),
        pltpu.VMEM((CHUNKS, 3, 4, 4, 16, 128), BF16),
        pltpu.VMEM((CHUNKS, 3, 4, 4, 16, 128), BF16),
        pltpu.VMEM((4, 2, 4, 16, 128), F32),
        pltpu.VMEM((4, 3, 4, 16, 128), F32),
        pltpu.VMEM((4, 3, 4, 16, 128), F32),
        pltpu.VMEM((3, 2, 4, 16, 128), BF16),
        pltpu.VMEM((3, 3, 4, 16, 128), BF16),
        pltpu.VMEM((3, 3, 4, 16, 128), BF16),
        pltpu.VMEM((3, 2, 4, 16, 128), BF16),
        pltpu.VMEM((3, 3, 4, 16, 128), BF16),
        pltpu.VMEM((3, 3, 4, 16, 128), BF16),
        pltpu.VMEM((4, 2, 16, 128), F32),
        pltpu.VMEM((3, 2, 16, 128), F32),
        pltpu.VMEM((4, 1, 2, 4, 128), F32),
        pltpu.VMEM((4, 3, 4, 4, 128), F32),
        pltpu.VMEM((4, 3, 4, 4, 128), F32),
        pltpu.VMEM((4, 1, 2, 4, 128), F32),
        pltpu.VMEM((4, 3, 4, 4, 128), F32),
        pltpu.VMEM((4, 3, 4, 4, 128), F32),
        pltpu.SemaphoreType.DMA((COPIES,)),
        pltpu.SemaphoreType.DMA((COPIES,)),
        pltpu.SemaphoreType.DMA((6,)),
    ]
    out = pl.pallas_call(
        kernel,
        out_shape=jax.ShapeDtypeStruct((4, 4224), F32),
        in_specs=[hbm] * 6,
        out_specs=pl.BlockSpec(memory_space=pltpu.VMEM),
        scratch_shapes=scratch,
        compiler_params=pltpu.CompilerParams(
            collective_id=0, has_side_effects=True, vmem_limit_bytes=60 << 20
        ),
        cost_estimate=pl.CostEstimate(flops=14495514624, bytes_accessed=19000000, transcendentals=1200000),
    )(student_hidden, teacher_hidden, student_head, teacher_head, group_counts, group_offsets)
    return out[:, 4096], out[:, :4096].astype(BF16)


def solution(mesh):
    both = ("wide", "narrow")
    return jax.shard_map(
        shards,
        mesh=mesh,
        in_specs=(P(both, None), P(both, None), P(None, both), P(None, both), P(), P()),
        out_specs=(P(both), P(both, None)),
        check_vma=False,
    )
```

```python
import jax
import jax.numpy as jnp
from jax import lax
from jax.experimental import pallas as pl
from jax.experimental.pallas import tpu as pltpu
from jax.sharding import PartitionSpec as P

MESH = pl.DeviceIdType.MESH
F32, BF16 = jnp.float32, jnp.bfloat16
AXES = ("z", "x", "y")
GATHER = ((0, 256, ("x", "y", "z")), (256, 384, ("y", "z", "x")), (640, 384, ("z", "x", "y")))
FIRST = ("z", "z", "x", "x", "x", "y", "y", "y")
THEN = {"z": "x", "x": "y", "y": "x"}
SEQUENCE = (2, 5, 0, 3, 6, 1, 4, 7)
CHUNKS = len(FIRST)
SENDS, ARRIVALS = 26, 73
FAR_FIRST = (2, 1, 3)
VOCAB = 1152
TILES = VOCAB // 128


def kernel(
    student_hbm, teacher_hbm, shead_hbm, thead_hbm, count_hbm, offset_hbm,
    out_ref,
    student_ref, teacher_ref, count_ref, offset_ref,
    shead, thead, rows, sl, tl, et, pd,
    pre_send, pre_recv, block, stat, st_send, st_recv,
    core_send, core_recv, own, stage0, recv0,
    curz, curx, cury, stagez, stagex, stagey, recvz, recvx, recvy, curz2, recvz2,
    finz, finx, finy, gotz, gotx, goty,
    send_sem, recv_sem, load_sem,
):
    wide = lax.axis_index("wide")
    me = {"z": lax.axis_index("narrow"), "x": wide // 8, "y": lax.rem(wide // 2, 4)}
    core = lax.rem(wide, 2)

    def device(at, c):
        return ((at["x"] * 4 + at["y"]) * 2 + c, at["z"])

    def shifted(axis, delta):
        return {**me, axis: lax.rem(me[axis] + delta, 4)}

    def peer(axis, delta):
        return device(shifted(axis, delta), core)

    sibling = device(me, 1 - core)
    sent, used = [], [0, 0]

    def fresh(kind):
        used[kind] += 1
        return used[kind] - 1

    def post(src, dst, to, leave, land):
        pltpu.make_async_remote_copy(
            src_ref=src, dst_ref=dst, send_sem=send_sem.at[leave], recv_sem=recv_sem.at[land],
            device_id=to, device_id_type=MESH,
        ).start()

    def landed(ref, land):
        pltpu.make_async_remote_copy(
            src_ref=ref, dst_ref=ref, send_sem=send_sem.at[0], recv_sem=recv_sem.at[land],
            device_id=sibling, device_id_type=MESH,
        ).wait_recv()

    def left(ref, leave):
        pltpu.make_async_remote_copy(
            src_ref=ref, dst_ref=ref, send_sem=send_sem.at[leave], recv_sem=recv_sem.at[0],
            device_id=sibling, device_id_type=MESH,
        ).wait_send()

    loads = [
        pltpu.make_async_copy(src, dst, load_sem.at[i])
        for i, (src, dst) in enumerate((
            (teacher_hbm, teacher_ref), (student_hbm, student_ref), (count_hbm, count_ref),
            (offset_hbm, offset_ref), (thead_hbm, thead), (shead_hbm, shead),
        ))
    ]
    for load in loads:
        load.start()

    barrier = pltpu.get_barrier_semaphore()
    friends = [peer(axis, delta) for axis in AXES for delta in (1, 2, 3)] + [sibling]
    for friend in friends:
        pl.semaphore_signal(barrier, inc=1, device_id=friend, device_id_type=MESH)

    for load in loads[:2]:
        load.wait()
    for q in range(4):
        pre_send[q, 0:4, :] = teacher_ref[:, q * 1024:(q + 1) * 1024].astype(F32)
        pre_send[q, 4:8, :] = student_ref[:, q * 1024:(q + 1) * 1024].astype(F32)
    pl.semaphore_wait(barrier, len(friends))

    z = me["z"]
    leave, land = fresh(0), fresh(1)
    for delta in FAR_FIRST:
        to = shifted("z", delta)
        post(pre_send.at[to["z"]], pre_recv.at[z], device(to, core), leave, land)
    pre_recv[z] = pre_send[z]
    sent.append((pre_send.at[pl.ds(0, 3)], leave))
    landed(pre_recv.at[pl.ds(0, 3)], land)
    for which in range(2):
        for s in range(4):
            block[4 * s:4 * s + 4, :] = pre_recv[s, 4 * which:4 * which + 4, :]
        rows[which, z, me["x"], me["y"], core] = block[...].astype(BF16)

    def region(part, free, at, c, which=None, half=None, wide_axis=None, count=3):
        start, width, order = GATHER[part]
        index = [pl.ds(0, 2) if which is None else which]
        for axis in AXES:
            if axis == wide_axis:
                index.append(pl.ds(0, count))
            elif axis not in free:
                index.append(at[axis])
            elif half is not None and axis == order[0]:
                index.append(pl.ds(2 * half, 2))
            else:
                index.append(pl.ds(0, 4))
        return rows.at[(*index, c, pl.ds(0, 16), pl.ds(start, width))]

    parts = range(len(GATHER))

    def spread(part, step):
        order = GATHER[part][2]
        here = region(part, order[:step], me, core)
        leave, land = fresh(0), fresh(1)
        for delta in FAR_FIRST:
            post(here, here, peer(order[step], delta), leave, land)
        three = region(part, order[:step], me, core, wide_axis=order[step])
        sent.append((three, leave))
        return three, land

    core_leave = [fresh(0) for _ in parts]
    last_leave = [fresh(0) for _ in parts]
    last_land = [[{name: fresh(1) for name in ("l0", "r1", "near", "far")} for _ in parts] for _ in range(2)]

    def to_core(part, at, land, which=None):
        here = region(part, GATHER[part][2][:2], at, core, which)
        post(here, here, sibling, core_leave[part], land)

    def start_last(which, names):
        for part in parts:
            order = GATHER[part][2]
            for name in names:
                here = region(part, order[:2], me, core, which, int(name[1]))
                land = last_land[which][part][name if name in ("l0", "r1") else "near"]
                post(here, here, peer(order[2], 1 if name[0] == "l" else 3), last_leave[part], land)

    def pass_on(which):
        for part in parts:
            order = GATHER[part][2]
            for name, delta, half, to in (("l0", 3, 0, 1), ("r1", 1, 1, 3)):
                here = region(part, order[:2], shifted(order[2], delta), core, which, half)
                landed(here, last_land[which][part][name])
                post(here, here, peer(order[2], to), last_leave[part], last_land[which][part]["far"])

    def box_to_core(which, name, deltas):
        arrivals = []
        for part in parts:
            axis, free = GATHER[part][2][2], GATHER[part][2][:2]
            landed(region(part, free, me, core, which), last_land[which][part][name])
            land = fresh(1)
            for delta in deltas:
                to_core(part, shifted(axis, delta), land, which)
            arrivals.append((region(part, free, me, core, which, wide_axis=axis, count=len(deltas)), land))
        return arrivals

    def near_to_core(which):
        return box_to_core(which, "near", (3, 1))

    def far_to_core(which):
        return box_to_core(which, "far", (2,))

    step0 = [spread(part, 0) for part in parts]
    step1 = []
    for part in parts:
        landed(*step0[part])
        step1.append(spread(part, 1))
    for part in parts:
        landed(*step1[part])
    start_last(0, ("l0", "r1", "l1", "r0"))
    start_last(1, ("l0", "r1"))
    own_core = []
    for part in parts:
        land = fresh(1)
        to_core(part, me, land)
        own_core.append((region(part, GATHER[part][2][:2], me, core), land))

    def logits(which, part, deltas, first=False):
        start, width, order = GATHER[part]
        axis = order[2]
        head, out = ((thead, tl), (shead, sl))[which]
        places = [shifted(axis, delta)[axis] for delta in deltas]
        cols = slice(start, start + width)
        if axis == "z":
            lhs = jnp.concatenate([rows[which, q, :, :, :, :, cols].reshape(512, width) for q in places], axis=1)
            tops = [pl.multiple_of(q * 1024 + start, 128) for q in places]
        else:
            lhs = jnp.concatenate([
                jnp.concatenate([
                    (rows[which, q, v, :, :, :, cols] if axis == "x" else rows[which, q, :, v, :, :, cols]).reshape(128, width)
                    for q in range(4)
                ], axis=1)
                for v in places
            ], axis=0)
            tops = [q * 1024 + start for q in range(4)]
        for tile in range(0, TILES, 2):
            count = min(2, TILES - tile)
            rhs = jnp.concatenate([head[pl.ds(top, width), tile * 128:(tile + count) * 128] for top in tops], axis=0)
            total = jnp.dot(lhs, rhs, preferred_element_type=F32)
            for i in range(count):
                piece = total[:, i * 128:(i + 1) * 128]
                if first:
                    out[tile + i] = piece
                elif axis == "z":
                    out[tile + i] += piece
                else:
                    for n, v in enumerate(places):
                        if axis == "x":
                            at = pl.ds(pl.multiple_of(v * 128, 128), 128)
                            out[tile + i, at, :] += piece[n * 128:(n + 1) * 128]
                        else:
                            for x in range(4):
                                at = pl.ds(pl.multiple_of(x * 128 + v * 32, 32), 32)
                                out[tile + i, at, :] += piece[n * 128 + x * 32:n * 128 + x * 32 + 32]

    def add_boxes(which, arrivals, deltas, first=False):
        for part in parts:
            landed(*arrivals[part])
            logits(which, part, deltas, first and part == 0)

    for load in loads[2:]:
        load.wait()
    add_boxes(0, own_core, (0,), True)
    pass_on(0)
    start_last(1, ("l1", "r0"))
    for part in parts:
        logits(1, part, (0,), part == 0)
    near = near_to_core(0)
    pass_on(1)
    add_boxes(0, near, (3, 1))
    far = far_to_core(0)
    near = near_to_core(1)
    add_boxes(0, far, (2,))
    far = far_to_core(1)
    add_boxes(1, near, (3, 1))
    add_boxes(1, far, (2,))
    for part in parts:
        order = GATHER[part][2]
        sent.append((region(part, order[:2], me, core, wide_axis=order[2]), last_leave[part]))
        sent.append((region(part, AXES, me, core), core_leave[part]))

    lane = lax.broadcasted_iota(jnp.int32, (64, 128), 1)

    def terms(b, carry):
        at = pl.ds(pl.multiple_of(b * 64, 64), 64)
        pairs = [pl.ds(offset_ref[b * 4 + i], 16) for i in range(4)]

        def paired(j):
            return jnp.concatenate([tl[j, pair, :] for pair in pairs], axis=0)

        smax, tmax = sl[0, at, :], paired(0)
        for j in range(1, TILES):
            smax = jnp.maximum(smax, sl[j, at, :])
            tmax = jnp.maximum(tmax, paired(j))
        smax = jnp.max(smax, axis=1, keepdims=True)
        tmax = jnp.max(tmax, axis=1, keepdims=True)
        ssum = tsum = cross = jnp.zeros((64, 128), F32)
        for j in range(TILES):
            s, t = sl[j, at, :], paired(j)
            e = jnp.exp(s - smax)
            sl[j, at, :] = e
            ssum = ssum + e
            e = jnp.exp(t - tmax)
            et[j, at, :] = e
            tsum = tsum + e
            cross = cross + e * (t - s)
        ssum = jnp.sum(ssum, axis=1, keepdims=True)
        tsum = jnp.sum(tsum, axis=1, keepdims=True)
        cross = jnp.sum(cross, axis=1, keepdims=True)
        tile = jnp.where(lane == 0, smax, jnp.where(lane == 1, tmax, jnp.where(lane == 2, ssum, jnp.where(lane == 3, tsum, cross))))
        stat[at, :] = tile
        return carry

    lax.fori_loop(0, 8, terms, 0)

    local = stat[...].T[0:8, :]
    now = local
    slot = 0
    for level, axis in enumerate(("core", "x", "y", "z")):
        st_send[level] = now
        if axis == "core":
            friends = [sibling]
        else:
            friends = [peer(axis, delta) for delta in FAR_FIRST]
        leave, land = fresh(0), fresh(1)
        for i, friend in enumerate(friends):
            post(st_send.at[level], st_recv.at[slot + i], friend, leave, land)
        landing = st_recv.at[pl.ds(slot, len(friends))]
        sent.append((landing, leave))
        landed(landing, land)
        members = [now] + [st_recv[slot + i] for i in range(len(friends))]
        slot += len(friends)
        smax, tmax = members[0][0:1], members[0][1:2]
        for member in members[1:]:
            smax = jnp.maximum(smax, member[0:1])
            tmax = jnp.maximum(tmax, member[1:2])
        ssum = tsum = cross = jnp.zeros((1, 512), F32)
        for member in members:
            a = jnp.exp(member[0:1] - smax)
            b = jnp.exp(member[1:2] - tmax)
            ssum = ssum + member[2:3] * a
            tsum = tsum + member[3:4] * b
            cross = cross + member[4:5] * b
        now = jnp.concatenate([smax, tmax, ssum, tsum, cross, cross, cross, cross], axis=0)
    value = cross / tsum - tmax - jnp.log(tsum) + smax + jnp.log(ssum)
    sscale = jnp.exp(local[0:1] - smax) / ssum
    tscale = jnp.exp(local[1:2] - tmax) / tsum
    filler = jnp.zeros((125, 512), F32)
    stat[...] = jnp.concatenate([sscale, tscale, value, filler], axis=0).T

    row = lax.broadcasted_iota(jnp.int32, (16, 128), 0)
    four = lax.broadcasted_iota(jnp.int32, (4, 128), 0)
    mine = stat[pl.ds(wide * 16 + z * 4, 4), :]
    mine = jnp.where(four + z * 4 < count_ref[wide], jnp.broadcast_to(mine[:, 2:3], (4, 128)), 0.0)
    out_ref[:, 4096:4224] = mine

    def prob_diff(pair, carry):
        for c in range(2):
            g = pair * 2 + c
            half = core if c else 1 - core
            at = pl.ds(pl.multiple_of(g * 16, 16), 16)
            scale = stat[at, :]
            live = row < count_ref[g]
            a = jnp.where(live, jnp.broadcast_to(scale[:, 0:1], (16, 128)), 0.0)
            b = jnp.where(live, jnp.broadcast_to(scale[:, 1:2], (16, 128)), 0.0)
            for j in range(TILES):
                pd[half, pair, :, j * 128:(j + 1) * 128] = (sl[j, at, :] * a - et[j, at, :] * b).astype(BF16)
        return carry

    lax.fori_loop(0, 16, prob_diff, 0)

    core_out, first_out = fresh(0), fresh(0)

    def grad_matmul(j):
        weights = jnp.concatenate([shead[q * 1024 + j * 128:q * 1024 + (j + 1) * 128, :] for q in range(4)], axis=0)
        out = lax.dot_general(
            pd[...].reshape(512, VOCAB), weights, (((1,), (1,)), ((), ())), preferred_element_type=F32
        )
        for q in range(4):
            piece = out[:, q * 128:(q + 1) * 128]
            core_send[j, q] = piece[0:256].astype(BF16).reshape(4, 4, 16, 128)
            own[j, q] = piece[256:512].reshape(4, 4, 16, 128)
        land = fresh(1)
        post(core_send.at[j], core_recv.at[j], sibling, core_out, land)
        return land

    def pick(ref, j, axis, q):
        index = [slice(None)] * 3
        index[AXES.index(axis)] = q
        return ref[(j, *index)]

    boxes = {}

    def first_start(j, core_land):
        axis = FIRST[j]
        landed(core_recv.at[j], core_land)
        boxes[j] = fresh(1)
        for i, delta in enumerate(FAR_FIRST):
            q = shifted(axis, delta)[axis]
            stage0[j, i] = (pick(own, j, axis, q) + pick(core_recv, j, axis, q).astype(F32)).astype(BF16)
            post(stage0.at[j, i], recv0.at[j, i], peer(axis, delta), first_out, boxes[j])

    cur = {"z": curz, "x": curx, "y": cury}
    stage = {"z": stagez, "x": stagex, "y": stagey}
    recv = {"z": recvz, "x": recvx, "y": recvy}

    def first_end(j):
        axis = FIRST[j]
        landed(recv0.at[j], boxes[j])
        total = pick(own, j, axis, me[axis]) + pick(core_recv, j, axis, me[axis]).astype(F32)
        for i in range(3):
            total = total + recv0[j, i].astype(F32)
        place = j - FIRST.index(axis)
        for q in range(4):
            cur[axis][q, place] = total[q] if axis == "z" else total[:, q]

    def second_start(axis):
        leave, land = fresh(0), fresh(1)
        for i, delta in enumerate(FAR_FIRST):
            q = shifted(THEN[axis], delta)[THEN[axis]]
            stage[axis][i] = cur[axis][q].astype(BF16)
            post(stage[axis].at[i], recv[axis].at[i], peer(THEN[axis], delta), leave, land)
        sent.append((stage[axis], leave))
        return land

    def second_end(axis, land):
        landed(recv[axis], land)
        total = cur[axis][me[THEN[axis]]]
        for i in range(3):
            total = total + recv[axis][i].astype(F32)
        return total

    def rows_start(total, fin, got):
        for q in range(4):
            fin[q] = total[:, :, 4 * q:4 * q + 4, :]
        leave, land = fresh(0), fresh(1)
        for delta in FAR_FIRST:
            q = shifted("z", delta)["z"]
            post(fin.at[q], got.at[z], peer("z", delta), leave, land)
        got[z] = fin[z]
        sent.append((fin.at[pl.ds(0, 3)], leave))
        return got.at[pl.ds(0, 3)], land

    waiting = []
    for n, j in enumerate(SEQUENCE):
        waiting.append((j, grad_matmul(j)))
        if n >= 1:
            first_start(*waiting.pop(0))
    first_start(*waiting.pop(0))

    sent += [(core_send, core_out), (stage0, first_out)]
    for j in (0, 1):
        first_end(j)
    zland = second_start("z")
    for j in (2, 3, 4):
        first_end(j)
    xland = second_start("x")
    for j in (5, 6, 7):
        first_end(j)
    yland = second_start("y")
    total = second_end("z", zland)
    for q in range(4):
        curz2[q] = total[:, q]
    leave, land = fresh(0), fresh(1)
    for i, delta in enumerate(FAR_FIRST):
        post(curz2.at[shifted("y", delta)["y"]], recvz2.at[i], peer("y", delta), leave, land)
    sent.append((recvz2, leave))
    xrows = rows_start(second_end("x", xland), finx, gotx)
    yrows = rows_start(second_end("y", yland), finy, goty)
    landed(recvz2, land)
    total = curz2[me["y"]] + recvz2[0] + recvz2[1] + recvz2[2]
    zrows = rows_start(total[None], finz, gotz)
    for axis, arrival, got in (("x", xrows, gotx), ("y", yrows, goty)):
        landed(*arrival)
        total = got[0] + got[1] + got[2] + got[3]
        for place in range(3):
            for q in range(4):
                at = q * 1024 + (FIRST.index(axis) + place) * 128
                out_ref[:, at:at + 128] = total[place, q]
    landed(*zrows)
    for place in range(2):
        for q in range(4):
            at = q * 1024 + place * 128
            out_ref[:, at:at + 128] = gotz[q, 0, place]
    for ref, leave in sent:
        left(ref, leave)
    assert tuple(used) == (SENDS, ARRIVALS), used


def shards(student_hidden, teacher_hidden, student_head, teacher_head, group_counts, group_offsets):
    hbm = pl.BlockSpec(memory_space=pl.ANY)
    head = pltpu.VMEM((4096, VOCAB), BF16)
    table = pltpu.VMEM((TILES, 512, 128), F32)
    scratch = [
        pltpu.VMEM((4, 4096), BF16),
        pltpu.VMEM((4, 4096), BF16),
        pltpu.SMEM((32,), jnp.int32),
        pltpu.SMEM((32,), jnp.int32),
        head, head,
        pltpu.VMEM((2, 4, 4, 4, 2, 16, 1024), BF16),
        table, table, table,
        pltpu.VMEM((2, 16, 16, VOCAB), BF16),
        pltpu.VMEM((4, 8, 1024), F32),
        pltpu.VMEM((4, 8, 1024), F32),
        pltpu.VMEM((16, 1024), F32),
        pltpu.VMEM((512, 128), F32),
        pltpu.VMEM((4, 8, 512), F32),
        pltpu.VMEM((10, 8, 512), F32),
        pltpu.VMEM((CHUNKS, 4, 4, 4, 16, 128), BF16),
        pltpu.VMEM((CHUNKS, 4, 4, 4, 16, 128), BF16),
        pltpu.VMEM((CHUNKS, 4, 4, 4, 16, 128), F32),
        pltpu.VMEM((CHUNKS, 3, 4, 4, 16, 128), BF16),
        pltpu.VMEM((CHUNKS, 3, 4, 4, 16, 128), BF16),
        pltpu.VMEM((4, 2, 4, 16, 128), F32),
        pltpu.VMEM((4, 3, 4, 16, 128), F32),
        pltpu.VMEM((4, 3, 4, 16, 128), F32),
        pltpu.VMEM((3, 2, 4, 16, 128), BF16),
        pltpu.VMEM((3, 3, 4, 16, 128), BF16),
        pltpu.VMEM((3, 3, 4, 16, 128), BF16),
        pltpu.VMEM((3, 2, 4, 16, 128), BF16),
        pltpu.VMEM((3, 3, 4, 16, 128), BF16),
        pltpu.VMEM((3, 3, 4, 16, 128), BF16),
        pltpu.VMEM((4, 2, 16, 128), F32),
        pltpu.VMEM((3, 2, 16, 128), F32),
        pltpu.VMEM((4, 1, 2, 4, 128), F32),
        pltpu.VMEM((4, 3, 4, 4, 128), F32),
        pltpu.VMEM((4, 3, 4, 4, 128), F32),
        pltpu.VMEM((4, 1, 2, 4, 128), F32),
        pltpu.VMEM((4, 3, 4, 4, 128), F32),
        pltpu.VMEM((4, 3, 4, 4, 128), F32),
        pltpu.SemaphoreType.DMA((SENDS,)),
        pltpu.SemaphoreType.DMA((ARRIVALS,)),
        pltpu.SemaphoreType.DMA((6,)),
    ]
    out = pl.pallas_call(
        kernel,
        out_shape=jax.ShapeDtypeStruct((4, 4224), F32),
        in_specs=[hbm] * 6,
        out_specs=pl.BlockSpec(memory_space=pltpu.VMEM),
        scratch_shapes=scratch,
        compiler_params=pltpu.CompilerParams(
            collective_id=0, has_side_effects=True, vmem_limit_bytes=60 << 20
        ),
        cost_estimate=pl.CostEstimate(flops=14495514624, bytes_accessed=19000000, transcendentals=1200000),
    )(student_hidden, teacher_hidden, student_head, teacher_head, group_counts, group_offsets)
    return out[:, 4096], out[:, :4096].astype(BF16)


def solution(mesh):
    both = ("wide", "narrow")
    return jax.shard_map(
        shards,
        mesh=mesh,
        in_specs=(P(both, None), P(both, None), P(None, both), P(None, both), P(), P()),
        out_specs=(P(both), P(both, None)),
        check_vma=False,
    )
```

```python
import jax
import jax.numpy as jnp
from jax import lax
from jax.experimental import pallas as pl
from jax.experimental.pallas import tpu as pltpu
from jax.sharding import PartitionSpec as P

MESH = pl.DeviceIdType.MESH
F32, BF16 = jnp.float32, jnp.bfloat16
AXES = ("z", "x", "y")
GATHER = ((0, 256, ("x", "y", "z")), (256, 384, ("y", "z", "x")), (640, 384, ("z", "x", "y")))
FIRST = ("z", "z", "x", "x", "x", "y", "y", "y")
THEN = {"z": "x", "x": "y", "y": "x"}
SEQUENCE = (2, 5, 0, 1, 3, 6, 4, 7)
LAG = 2
PLANE = sorted(((a, b) for a in range(4) for b in range(4) if a or b), key=lambda d: -sum(min(e, 4 - e) for e in d))
CHUNKS = len(FIRST)
SENDS, ARRIVALS = 24, 71
FAR_FIRST = (2, 1, 3)
VOCAB = 1152
TILES = VOCAB // 128


def kernel(
    student_hbm, teacher_hbm, shead_hbm, thead_hbm, count_hbm, offset_hbm,
    out_ref,
    student_ref, teacher_ref, count_ref, offset_ref,
    shead, thead, rows, sl, tl, et, pd,
    pre_send, pre_recv, pack, block, stat, st_send, st_recv,
    core_send, core_recv, own, stage0, recv0,
    curz, curx, cury, stagez, stagex, stagey, recvz, recvx, recvy, curz2, recvz2,
    finz, finx, finy, gotz, gotx, goty,
    send_sem, recv_sem, load_sem,
):
    wide = lax.axis_index("wide")
    me = {"z": lax.axis_index("narrow"), "x": wide // 8, "y": lax.rem(wide // 2, 4)}
    core = lax.rem(wide, 2)

    def device(at, c):
        return ((at["x"] * 4 + at["y"]) * 2 + c, at["z"])

    def shifted(axis, delta):
        return {**me, axis: lax.rem(me[axis] + delta, 4)}

    def peer(axis, delta):
        return device(shifted(axis, delta), core)

    sibling = device(me, 1 - core)
    sent, used = [], [0, 0]

    def fresh(kind):
        used[kind] += 1
        return used[kind] - 1

    def post(src, dst, to, leave, land):
        pltpu.make_async_remote_copy(
            src_ref=src, dst_ref=dst, send_sem=send_sem.at[leave], recv_sem=recv_sem.at[land],
            device_id=to, device_id_type=MESH,
        ).start()

    def landed(ref, land):
        pltpu.make_async_remote_copy(
            src_ref=ref, dst_ref=ref, send_sem=send_sem.at[0], recv_sem=recv_sem.at[land],
            device_id=sibling, device_id_type=MESH,
        ).wait_recv()

    def left(ref, leave):
        pltpu.make_async_remote_copy(
            src_ref=ref, dst_ref=ref, send_sem=send_sem.at[leave], recv_sem=recv_sem.at[0],
            device_id=sibling, device_id_type=MESH,
        ).wait_send()

    loads = [
        pltpu.make_async_copy(src, dst, load_sem.at[i])
        for i, (src, dst) in enumerate((
            (teacher_hbm, teacher_ref), (student_hbm, student_ref), (count_hbm, count_ref),
            (offset_hbm, offset_ref), (thead_hbm, thead), (shead_hbm, shead),
        ))
    ]
    for load in loads:
        load.start()

    barrier = pltpu.get_barrier_semaphore()
    friends = [peer(axis, delta) for axis in AXES for delta in (1, 2, 3)] + [sibling]
    for friend in friends:
        pl.semaphore_signal(barrier, inc=1, device_id=friend, device_id_type=MESH)

    for load in loads[:2]:
        load.wait()
    for q in range(4):
        for h in range(2):
            at = slice(q * 1024 + h * 512, q * 1024 + h * 512 + 512)
            pack[q, 4 * h:4 * h + 4, :] = teacher_ref[:, at].astype(F32)
            pack[q, 8 + 4 * h:12 + 4 * h, :] = student_ref[:, at].astype(F32)
    pre_send[...] = pack[...].astype(BF16)
    pl.semaphore_wait(barrier, len(friends))

    z = me["z"]
    leave, land = fresh(0), fresh(1)
    for delta in FAR_FIRST:
        to = shifted("z", delta)
        post(pre_send.at[to["z"]], pre_recv.at[z], device(to, core), leave, land)
    pre_recv[z] = pre_send[z]
    sent.append((pre_send.at[pl.ds(0, 3)], leave))
    landed(pre_recv.at[pl.ds(0, 3)], land)
    pack[...] = pre_recv[...].astype(F32)
    for which in range(2):
        for s in range(4):
            for h in range(2):
                top = 8 * which + 4 * h
                block[4 * s:4 * s + 4, h * 512:h * 512 + 512] = pack[s, top:top + 4, :]
        rows[which, z, me["x"], me["y"], core] = block[...].astype(BF16)

    def region(part, free, at, c, which=None, half=None, wide_axis=None, count=3):
        start, width, order = GATHER[part]
        index = [pl.ds(0, 2) if which is None else which]
        for axis in AXES:
            if axis == wide_axis:
                index.append(pl.ds(0, count))
            elif axis not in free:
                index.append(at[axis])
            elif half is not None and axis == order[0]:
                index.append(pl.ds(2 * half, 2))
            else:
                index.append(pl.ds(0, 4))
        return rows.at[(*index, c, pl.ds(0, 16), pl.ds(start, width))]

    parts = range(len(GATHER))

    def spread(part, step):
        order = GATHER[part][2]
        here = region(part, order[:step], me, core)
        leave, land = fresh(0), fresh(1)
        for delta in FAR_FIRST:
            post(here, here, peer(order[step], delta), leave, land)
        three = region(part, order[:step], me, core, wide_axis=order[step])
        sent.append((three, leave))
        return three, land

    core_leave = [fresh(0) for _ in parts]
    last_leave = [fresh(0) for _ in parts]
    last_land = [[{name: fresh(1) for name in ("l0", "r1", "near", "far")} for _ in parts] for _ in range(2)]

    def to_core(part, at, land, which=None):
        here = region(part, GATHER[part][2][:2], at, core, which)
        post(here, here, sibling, core_leave[part], land)

    def start_last(which, names):
        for part in parts:
            order = GATHER[part][2]
            for name in names:
                here = region(part, order[:2], me, core, which, int(name[1]))
                land = last_land[which][part][name if name in ("l0", "r1") else "near"]
                post(here, here, peer(order[2], 1 if name[0] == "l" else 3), last_leave[part], land)

    def pass_on(which):
        for part in parts:
            order = GATHER[part][2]
            for name, delta, half, to in (("l0", 3, 0, 1), ("r1", 1, 1, 3)):
                here = region(part, order[:2], shifted(order[2], delta), core, which, half)
                landed(here, last_land[which][part][name])
                post(here, here, peer(order[2], to), last_leave[part], last_land[which][part]["far"])

    def box_to_core(which, name, deltas):
        arrivals = []
        for part in parts:
            axis, free = GATHER[part][2][2], GATHER[part][2][:2]
            landed(region(part, free, me, core, which), last_land[which][part][name])
            land = fresh(1)
            for delta in deltas:
                to_core(part, shifted(axis, delta), land, which)
            arrivals.append((region(part, free, me, core, which, wide_axis=axis, count=len(deltas)), land))
        return arrivals

    def near_to_core(which):
        return box_to_core(which, "near", (3, 1))

    def far_to_core(which):
        return box_to_core(which, "far", (2,))

    step0 = [spread(part, 0) for part in parts]
    step1 = []
    for part in parts:
        landed(*step0[part])
        step1.append(spread(part, 1))
    for part in parts:
        landed(*step1[part])
    start_last(0, ("l0", "r1", "l1", "r0"))
    start_last(1, ("l0", "r1"))
    own_core = []
    for part in parts:
        land = fresh(1)
        to_core(part, me, land)
        own_core.append((region(part, GATHER[part][2][:2], me, core), land))

    def logits(which, part, deltas, first=False):
        start, width, order = GATHER[part]
        axis = order[2]
        head, out = ((thead, tl), (shead, sl))[which]
        places = [shifted(axis, delta)[axis] for delta in deltas]
        cols = slice(start, start + width)
        if axis == "z":
            lhs = jnp.concatenate([rows[which, q, :, :, :, :, cols].reshape(512, width) for q in places], axis=1)
            tops = [pl.multiple_of(q * 1024 + start, 128) for q in places]
        else:
            lhs = jnp.concatenate([
                jnp.concatenate([
                    (rows[which, q, v, :, :, :, cols] if axis == "x" else rows[which, q, :, v, :, :, cols]).reshape(128, width)
                    for q in range(4)
                ], axis=1)
                for v in places
            ], axis=0)
            tops = [q * 1024 + start for q in range(4)]
        for tile in range(0, TILES, 2):
            count = min(2, TILES - tile)
            rhs = jnp.concatenate([head[pl.ds(top, width), tile * 128:(tile + count) * 128] for top in tops], axis=0)
            total = jnp.dot(lhs, rhs, preferred_element_type=F32)
            for i in range(count):
                piece = total[:, i * 128:(i + 1) * 128]
                if first:
                    out[tile + i] = piece
                elif axis == "z":
                    out[tile + i] += piece
                else:
                    for n, v in enumerate(places):
                        if axis == "x":
                            at = pl.ds(pl.multiple_of(v * 128, 128), 128)
                            out[tile + i, at, :] += piece[n * 128:(n + 1) * 128]
                        else:
                            for x in range(4):
                                at = pl.ds(pl.multiple_of(x * 128 + v * 32, 32), 32)
                                out[tile + i, at, :] += piece[n * 128 + x * 32:n * 128 + x * 32 + 32]

    def add_boxes(which, arrivals, deltas, first=False):
        for part in parts:
            landed(*arrivals[part])
            logits(which, part, deltas, first and part == 0)

    for load in loads[2:]:
        load.wait()
    add_boxes(0, own_core, (0,), True)
    pass_on(0)
    start_last(1, ("l1", "r0"))
    for part in parts:
        logits(1, part, (0,), part == 0)
    near = near_to_core(0)
    pass_on(1)
    add_boxes(0, near, (3, 1))
    far = far_to_core(0)
    near = near_to_core(1)
    add_boxes(0, far, (2,))
    far = far_to_core(1)
    add_boxes(1, near, (3, 1))
    add_boxes(1, far, (2,))
    for part in parts:
        order = GATHER[part][2]
        sent.append((region(part, order[:2], me, core, wide_axis=order[2]), last_leave[part]))
        sent.append((region(part, AXES, me, core), core_leave[part]))

    lane = lax.broadcasted_iota(jnp.int32, (64, 128), 1)

    def terms(b, carry):
        at = pl.ds(pl.multiple_of(b * 64, 64), 64)
        pairs = [pl.ds(offset_ref[b * 4 + i], 16) for i in range(4)]

        def paired(j):
            return jnp.concatenate([tl[j, pair, :] for pair in pairs], axis=0)

        smax, tmax = sl[0, at, :], paired(0)
        for j in range(1, TILES):
            smax = jnp.maximum(smax, sl[j, at, :])
            tmax = jnp.maximum(tmax, paired(j))
        smax = jnp.max(smax, axis=1, keepdims=True)
        tmax = jnp.max(tmax, axis=1, keepdims=True)
        ssum = tsum = cross = jnp.zeros((64, 128), F32)
        for j in range(TILES):
            s, t = sl[j, at, :], paired(j)
            e = jnp.exp(s - smax)
            sl[j, at, :] = e
            ssum = ssum + e
            e = jnp.exp(t - tmax)
            et[j, at, :] = e
            tsum = tsum + e
            cross = cross + e * (t - s)
        ssum = jnp.sum(ssum, axis=1, keepdims=True)
        tsum = jnp.sum(tsum, axis=1, keepdims=True)
        cross = jnp.sum(cross, axis=1, keepdims=True)
        tile = jnp.where(lane == 0, smax, jnp.where(lane == 1, tmax, jnp.where(lane == 2, ssum, jnp.where(lane == 3, tsum, cross))))
        stat[at, :] = tile
        return carry

    lax.fori_loop(0, 8, terms, 0)

    local = stat[...].T[0:8, :]
    now = local
    slot = 0
    for level in range(2):
        st_send[level] = now
        if level == 0:
            friends = [device(shifted("x", delta), c) for delta in FAR_FIRST for c in (1 - core, core)] + [sibling]
        else:
            friends = [device({**shifted("y", a), "z": shifted("z", b)["z"]}, core) for a, b in PLANE]
        leave, land = fresh(0), fresh(1)
        for i, friend in enumerate(friends):
            post(st_send.at[level], st_recv.at[slot + i], friend, leave, land)
        landing = st_recv.at[pl.ds(slot, len(friends))]
        sent.append((landing, leave))
        landed(landing, land)
        members = [now] + [st_recv[slot + i] for i in range(len(friends))]
        slot += len(friends)
        smax, tmax = members[0][0:1], members[0][1:2]
        for member in members[1:]:
            smax = jnp.maximum(smax, member[0:1])
            tmax = jnp.maximum(tmax, member[1:2])
        ssum = tsum = cross = jnp.zeros((1, 512), F32)
        for member in members:
            a = jnp.exp(member[0:1] - smax)
            b = jnp.exp(member[1:2] - tmax)
            ssum = ssum + member[2:3] * a
            tsum = tsum + member[3:4] * b
            cross = cross + member[4:5] * b
        now = jnp.concatenate([smax, tmax, ssum, tsum, cross, cross, cross, cross], axis=0)
    value = cross / tsum - tmax - jnp.log(tsum) + smax + jnp.log(ssum)
    sscale = jnp.exp(local[0:1] - smax) / ssum
    tscale = jnp.exp(local[1:2] - tmax) / tsum
    filler = jnp.zeros((125, 512), F32)
    stat[...] = jnp.concatenate([sscale, tscale, value, filler], axis=0).T

    row = lax.broadcasted_iota(jnp.int32, (16, 128), 0)
    four = lax.broadcasted_iota(jnp.int32, (4, 128), 0)
    mine = stat[pl.ds(wide * 16 + z * 4, 4), :]
    mine = jnp.where(four + z * 4 < count_ref[wide], jnp.broadcast_to(mine[:, 2:3], (4, 128)), 0.0)
    out_ref[:, 4096:4224] = mine

    def prob_diff(pair, carry):
        for c in range(2):
            g = pair * 2 + c
            half = core if c else 1 - core
            at = pl.ds(pl.multiple_of(g * 16, 16), 16)
            scale = stat[at, :]
            live = row < count_ref[g]
            a = jnp.where(live, jnp.broadcast_to(scale[:, 0:1], (16, 128)), 0.0)
            b = jnp.where(live, jnp.broadcast_to(scale[:, 1:2], (16, 128)), 0.0)
            for j in range(TILES):
                pd[half, pair, :, j * 128:(j + 1) * 128] = (sl[j, at, :] * a - et[j, at, :] * b).astype(BF16)
        return carry

    lax.fori_loop(0, 16, prob_diff, 0, unroll=4)

    core_out, first_out = fresh(0), fresh(0)

    def grad_matmul(j):
        weights = jnp.concatenate([shead[q * 1024 + j * 128:q * 1024 + (j + 1) * 128, :] for q in range(4)], axis=0)
        out = lax.dot_general(
            pd[...].reshape(512, VOCAB), weights, (((1,), (1,)), ((), ())), preferred_element_type=F32
        )
        for q in range(4):
            piece = out[:, q * 128:(q + 1) * 128]
            core_send[j, q] = piece[0:256].astype(BF16).reshape(4, 4, 16, 128)
            own[j, q] = piece[256:512].reshape(4, 4, 16, 128)
    def pick(ref, j, axis, q):
        index = [slice(None)] * 3
        index[AXES.index(axis)] = q
        return ref[(j, *index)]

    boxes = {}

    def first_stage(j, core_land):
        axis = FIRST[j]
        landed(core_recv.at[j], core_land)
        for i, delta in enumerate(FAR_FIRST):
            q = shifted(axis, delta)[axis]
            stage0[j, i] = (pick(own, j, axis, q) + pick(core_recv, j, axis, q).astype(F32)).astype(BF16)

    def first_start(j):
        boxes[j] = fresh(1)
        for i, delta in enumerate(FAR_FIRST):
            post(stage0.at[j, i], recv0.at[j, i], peer(FIRST[j], delta), first_out, boxes[j])

    cur = {"z": curz, "x": curx, "y": cury}
    stage = {"z": stagez, "x": stagex, "y": stagey}
    recv = {"z": recvz, "x": recvx, "y": recvy}

    def first_end(j):
        axis = FIRST[j]
        landed(recv0.at[j], boxes[j])
        total = pick(own, j, axis, me[axis]) + pick(core_recv, j, axis, me[axis]).astype(F32)
        for i in range(3):
            total = total + recv0[j, i].astype(F32)
        place = j - FIRST.index(axis)
        for q in range(4):
            cur[axis][q, place] = total[q] if axis == "z" else total[:, q]

    def second_start(axis):
        leave, land = fresh(0), fresh(1)
        for i, delta in enumerate(FAR_FIRST):
            q = shifted(THEN[axis], delta)[THEN[axis]]
            stage[axis][i] = cur[axis][q].astype(BF16)
            post(stage[axis].at[i], recv[axis].at[i], peer(THEN[axis], delta), leave, land)
        sent.append((stage[axis], leave))
        return land

    def second_end(axis, land):
        landed(recv[axis], land)
        total = cur[axis][me[THEN[axis]]]
        for i in range(3):
            total = total + recv[axis][i].astype(F32)
        return total

    def rows_start(total, fin, got):
        for q in range(4):
            fin[q] = total[:, :, 4 * q:4 * q + 4, :]
        leave, land = fresh(0), fresh(1)
        for delta in FAR_FIRST:
            q = shifted("z", delta)["z"]
            post(fin.at[q], got.at[z], peer("z", delta), leave, land)
        got[z] = fin[z]
        sent.append((fin.at[pl.ds(0, 3)], leave))
        return got.at[pl.ds(0, 3)], land

    core_land = {}
    for n in range(CHUNKS + LAG):
        if n < CHUNKS:
            j = SEQUENCE[n]
            grad_matmul(j)
            core_land[j] = fresh(1)
            post(core_send.at[j], core_recv.at[j], sibling, core_out, core_land[j])
        if n >= LAG:
            first_stage(SEQUENCE[n - LAG], core_land[SEQUENCE[n - LAG]])
            first_start(SEQUENCE[n - LAG])

    sent += [(core_send, core_out), (stage0, first_out)]
    for j in (0, 1):
        first_end(j)
    zland = second_start("z")
    for j in (2, 5, 3, 6, 4):
        first_end(j)
    xland = second_start("x")
    first_end(7)
    yland = second_start("y")
    total = second_end("z", zland)
    for q in range(4):
        curz2[q] = total[:, q]
    leave, land = fresh(0), fresh(1)
    for i, delta in enumerate(FAR_FIRST):
        post(curz2.at[shifted("y", delta)["y"]], recvz2.at[i], peer("y", delta), leave, land)
    sent.append((recvz2, leave))
    xrows = rows_start(second_end("x", xland), finx, gotx)
    yrows = rows_start(second_end("y", yland), finy, goty)
    landed(recvz2, land)
    total = curz2[me["y"]] + recvz2[0] + recvz2[1] + recvz2[2]
    zrows = rows_start(total[None], finz, gotz)
    for axis, arrival, got in (("x", xrows, gotx), ("y", yrows, goty)):
        landed(*arrival)
        total = got[0] + got[1] + got[2] + got[3]
        for place in range(3):
            for q in range(4):
                at = q * 1024 + (FIRST.index(axis) + place) * 128
                out_ref[:, at:at + 128] = total[place, q]
    landed(*zrows)
    for place in range(2):
        for q in range(4):
            at = q * 1024 + place * 128
            out_ref[:, at:at + 128] = gotz[q, 0, place]
    for ref, leave in sent:
        left(ref, leave)
    assert tuple(used) == (SENDS, ARRIVALS), used


def shards(student_hidden, teacher_hidden, student_head, teacher_head, group_counts, group_offsets):
    hbm = pl.BlockSpec(memory_space=pl.ANY)
    head = pltpu.VMEM((4096, VOCAB), BF16)
    table = pltpu.VMEM((TILES, 512, 128), F32)
    scratch = [
        pltpu.VMEM((4, 4096), BF16),
        pltpu.VMEM((4, 4096), BF16),
        pltpu.SMEM((32,), jnp.int32),
        pltpu.SMEM((32,), jnp.int32),
        head, head,
        pltpu.VMEM((2, 4, 4, 4, 2, 16, 1024), BF16),
        table, table, table,
        pltpu.VMEM((2, 16, 16, VOCAB), BF16),
        pltpu.VMEM((4, 16, 512), BF16),
        pltpu.VMEM((4, 16, 512), BF16),
        pltpu.VMEM((4, 16, 512), F32),
        pltpu.VMEM((16, 1024), F32),
        pltpu.VMEM((512, 128), F32),
        pltpu.VMEM((2, 8, 512), F32),
        pltpu.VMEM((22, 8, 512), F32),
        pltpu.VMEM((CHUNKS, 4, 4, 4, 16, 128), BF16),
        pltpu.VMEM((CHUNKS, 4, 4, 4, 16, 128), BF16),
        pltpu.VMEM((CHUNKS, 4, 4, 4, 16, 128), F32),
        pltpu.VMEM((CHUNKS, 3, 4, 4, 16, 128), BF16),
        pltpu.VMEM((CHUNKS, 3, 4, 4, 16, 128), BF16),
        pltpu.VMEM((4, 2, 4, 16, 128), F32),
        pltpu.VMEM((4, 3, 4, 16, 128), F32),
        pltpu.VMEM((4, 3, 4, 16, 128), F32),
        pltpu.VMEM((3, 2, 4, 16, 128), BF16),
        pltpu.VMEM((3, 3, 4, 16, 128), BF16),
        pltpu.VMEM((3, 3, 4, 16, 128), BF16),
        pltpu.VMEM((3, 2, 4, 16, 128), BF16),
        pltpu.VMEM((3, 3, 4, 16, 128), BF16),
        pltpu.VMEM((3, 3, 4, 16, 128), BF16),
        pltpu.VMEM((4, 2, 16, 128), F32),
        pltpu.VMEM((3, 2, 16, 128), F32),
        pltpu.VMEM((4, 1, 2, 4, 128), F32),
        pltpu.VMEM((4, 3, 4, 4, 128), F32),
        pltpu.VMEM((4, 3, 4, 4, 128), F32),
        pltpu.VMEM((4, 1, 2, 4, 128), F32),
        pltpu.VMEM((4, 3, 4, 4, 128), F32),
        pltpu.VMEM((4, 3, 4, 4, 128), F32),
        pltpu.SemaphoreType.DMA((SENDS,)),
        pltpu.SemaphoreType.DMA((ARRIVALS,)),
        pltpu.SemaphoreType.DMA((6,)),
    ]
    out = pl.pallas_call(
        kernel,
        out_shape=jax.ShapeDtypeStruct((4, 4224), F32),
        in_specs=[hbm] * 6,
        out_specs=pl.BlockSpec(memory_space=pltpu.VMEM),
        scratch_shapes=scratch,
        compiler_params=pltpu.CompilerParams(
            collective_id=0, has_side_effects=True, vmem_limit_bytes=60 << 20
        ),
        cost_estimate=pl.CostEstimate(flops=14495514624, bytes_accessed=19000000, transcendentals=1200000),
    )(student_hidden, teacher_hidden, student_head, teacher_head, group_counts, group_offsets)
    return out[:, 4096], out[:, :4096].astype(BF16)


def solution(mesh):
    both = ("wide", "narrow")
    return jax.shard_map(
        shards,
        mesh=mesh,
        in_specs=(P(both, None), P(both, None), P(None, both), P(None, both), P(), P()),
        out_specs=(P(both), P(both, None)),
        check_vma=False,
    )
```

```python
import jax
import jax.numpy as jnp
from jax import lax
from jax.experimental import pallas as pl
from jax.experimental.pallas import tpu as pltpu
from jax.sharding import PartitionSpec as P

MESH = pl.DeviceIdType.MESH
F32, BF16 = jnp.float32, jnp.bfloat16
AXES = ("z", "x", "y")
GATHER = ((0, 256, ("x", "y", "z")), (256, 384, ("y", "z", "x")), (640, 384, ("z", "x", "y")))
FIRST = ("z", "z", "x", "x", "x", "y", "y", "y")
THEN = {"z": "x", "x": "y", "y": "x"}
SEQUENCE = (2, 5, 0, 1, 3, 6, 4, 7)
LAG = 2
PLANE = sorted(((a, b) for a in range(4) for b in range(4) if a or b), key=lambda d: -sum(min(e, 4 - e) for e in d))
CHUNKS = len(FIRST)
SENDS, ARRIVALS = 24, 71
FAR_FIRST = (2, 1, 3)
VOCAB = 1152
TILES = VOCAB // 128


def kernel(
    student_hbm, teacher_hbm, shead_hbm, thead_hbm, count_hbm, offset_hbm,
    out_ref,
    student_ref, teacher_ref, count_ref, offset_ref,
    shead, thead, rows, sl, tl, et, pd,
    pre_send, pre_recv, pack, block, stat, st_send, st_recv,
    core_send, core_recv, own, stage0, recv0,
    curz, curx, cury, stagez, stagex, stagey, recvz, recvx, recvy, curz2, recvz2,
    finz, finx, finy, gotz, gotx, goty,
    send_sem, recv_sem, load_sem,
):
    wide = lax.axis_index("wide")
    me = {"z": lax.axis_index("narrow"), "x": wide // 8, "y": lax.rem(wide // 2, 4)}
    core = lax.rem(wide, 2)

    def device(at, c):
        return ((at["x"] * 4 + at["y"]) * 2 + c, at["z"])

    def shifted(axis, delta):
        return {**me, axis: lax.rem(me[axis] + delta, 4)}

    def peer(axis, delta):
        return device(shifted(axis, delta), core)

    sibling = device(me, 1 - core)
    sent, used = [], [0, 0]

    def fresh(kind):
        used[kind] += 1
        return used[kind] - 1

    def post(src, dst, to, leave, land):
        pltpu.make_async_remote_copy(
            src_ref=src, dst_ref=dst, send_sem=send_sem.at[leave], recv_sem=recv_sem.at[land],
            device_id=to, device_id_type=MESH,
        ).start()

    def landed(ref, land):
        pltpu.make_async_remote_copy(
            src_ref=ref, dst_ref=ref, send_sem=send_sem.at[0], recv_sem=recv_sem.at[land],
            device_id=sibling, device_id_type=MESH,
        ).wait_recv()

    def left(ref, leave):
        pltpu.make_async_remote_copy(
            src_ref=ref, dst_ref=ref, send_sem=send_sem.at[leave], recv_sem=recv_sem.at[0],
            device_id=sibling, device_id_type=MESH,
        ).wait_send()

    loads = [
        pltpu.make_async_copy(src, dst, load_sem.at[i])
        for i, (src, dst) in enumerate((
            (teacher_hbm, teacher_ref), (student_hbm, student_ref), (count_hbm, count_ref),
            (offset_hbm, offset_ref), (thead_hbm, thead), (shead_hbm, shead),
        ))
    ]
    for load in loads:
        load.start()

    barrier = pltpu.get_barrier_semaphore()
    friends = [peer(axis, delta) for axis in AXES for delta in (1, 2, 3)] + [sibling]
    for friend in friends:
        pl.semaphore_signal(barrier, inc=1, device_id=friend, device_id_type=MESH)

    for load in loads[:2]:
        load.wait()
    for q in range(4):
        for h in range(2):
            at = slice(q * 1024 + h * 512, q * 1024 + h * 512 + 512)
            pack[q, 4 * h:4 * h + 4, :] = teacher_ref[:, at].astype(F32)
            pack[q, 8 + 4 * h:12 + 4 * h, :] = student_ref[:, at].astype(F32)
    pre_send[...] = pack[...].astype(BF16)
    pl.semaphore_wait(barrier, len(friends))

    z = me["z"]
    leave, land = fresh(0), fresh(1)
    for delta in FAR_FIRST:
        to = shifted("z", delta)
        post(pre_send.at[to["z"]], pre_recv.at[z], device(to, core), leave, land)
    pre_recv[z] = pre_send[z]
    sent.append((pre_send.at[pl.ds(0, 3)], leave))
    landed(pre_recv.at[pl.ds(0, 3)], land)
    pack[...] = pre_recv[...].astype(F32)
    for which in range(2):
        for s in range(4):
            for h in range(2):
                top = 8 * which + 4 * h
                block[4 * s:4 * s + 4, h * 512:h * 512 + 512] = pack[s, top:top + 4, :]
        rows[which, z, me["x"], me["y"], core] = block[...].astype(BF16)

    def region(part, free, at, c, which=None, half=None, wide_axis=None, count=3):
        start, width, order = GATHER[part]
        index = [pl.ds(0, 2) if which is None else which]
        for axis in AXES:
            if axis == wide_axis:
                index.append(pl.ds(0, count))
            elif axis not in free:
                index.append(at[axis])
            elif half is not None and axis == order[0]:
                index.append(pl.ds(2 * half, 2))
            else:
                index.append(pl.ds(0, 4))
        return rows.at[(*index, c, pl.ds(0, 16), pl.ds(start, width))]

    parts = range(len(GATHER))

    def spread(part, step):
        order = GATHER[part][2]
        here = region(part, order[:step], me, core)
        leave, land = fresh(0), fresh(1)
        for delta in FAR_FIRST:
            post(here, here, peer(order[step], delta), leave, land)
        three = region(part, order[:step], me, core, wide_axis=order[step])
        sent.append((three, leave))
        return three, land

    core_leave = [fresh(0) for _ in parts]
    last_leave = [fresh(0) for _ in parts]
    last_land = [[{name: fresh(1) for name in ("l0", "r1", "near", "far")} for _ in parts] for _ in range(2)]

    def to_core(part, at, land, which=None):
        here = region(part, GATHER[part][2][:2], at, core, which)
        post(here, here, sibling, core_leave[part], land)

    def start_last(which, names):
        for part in parts:
            order = GATHER[part][2]
            for name in names:
                here = region(part, order[:2], me, core, which, int(name[1]))
                land = last_land[which][part][name if name in ("l0", "r1") else "near"]
                post(here, here, peer(order[2], 1 if name[0] == "l" else 3), last_leave[part], land)

    def pass_on(which):
        for part in parts:
            order = GATHER[part][2]
            for name, delta, half, to in (("l0", 3, 0, 1), ("r1", 1, 1, 3)):
                here = region(part, order[:2], shifted(order[2], delta), core, which, half)
                landed(here, last_land[which][part][name])
                post(here, here, peer(order[2], to), last_leave[part], last_land[which][part]["far"])

    def box_to_core(which, name, deltas):
        arrivals = []
        for part in parts:
            axis, free = GATHER[part][2][2], GATHER[part][2][:2]
            landed(region(part, free, me, core, which), last_land[which][part][name])
            land = fresh(1)
            for delta in deltas:
                to_core(part, shifted(axis, delta), land, which)
            arrivals.append((region(part, free, me, core, which, wide_axis=axis, count=len(deltas)), land))
        return arrivals

    def near_to_core(which):
        return box_to_core(which, "near", (3, 1))

    def far_to_core(which):
        return box_to_core(which, "far", (2,))

    step0 = [spread(part, 0) for part in parts]
    step1 = []
    for part in parts:
        landed(*step0[part])
        step1.append(spread(part, 1))
    for part in parts:
        landed(*step1[part])
    start_last(0, ("l0", "r1", "l1", "r0"))
    start_last(1, ("l0", "r1"))
    own_core = []
    for part in parts:
        land = fresh(1)
        to_core(part, me, land)
        own_core.append((region(part, GATHER[part][2][:2], me, core), land))

    def logits(which, part, deltas, first=False):
        start, width, order = GATHER[part]
        axis = order[2]
        head, out = ((thead, tl), (shead, sl))[which]
        places = [shifted(axis, delta)[axis] for delta in deltas]
        cols = slice(start, start + width)
        if axis == "z":
            lhs = jnp.concatenate([rows[which, q, :, :, :, :, cols].reshape(512, width) for q in places], axis=1)
            tops = [pl.multiple_of(q * 1024 + start, 128) for q in places]
        else:
            lhs = jnp.concatenate([
                jnp.concatenate([
                    (rows[which, q, v, :, :, :, cols] if axis == "x" else rows[which, q, :, v, :, :, cols]).reshape(128, width)
                    for q in range(4)
                ], axis=1)
                for v in places
            ], axis=0)
            tops = [q * 1024 + start for q in range(4)]
        for tile in range(0, TILES, 2):
            count = min(2, TILES - tile)
            rhs = jnp.concatenate([head[pl.ds(top, width), tile * 128:(tile + count) * 128] for top in tops], axis=0)
            total = jnp.dot(lhs, rhs, preferred_element_type=F32)
            for i in range(count):
                piece = total[:, i * 128:(i + 1) * 128]
                if first:
                    out[tile + i] = piece
                elif axis == "z":
                    out[tile + i] += piece
                else:
                    for n, v in enumerate(places):
                        if axis == "x":
                            at = pl.ds(pl.multiple_of(v * 128, 128), 128)
                            out[tile + i, at, :] += piece[n * 128:(n + 1) * 128]
                        else:
                            for x in range(4):
                                at = pl.ds(pl.multiple_of(x * 128 + v * 32, 32), 32)
                                out[tile + i, at, :] += piece[n * 128 + x * 32:n * 128 + x * 32 + 32]

    def add_boxes(which, arrivals, deltas, first=False):
        for part in parts:
            landed(*arrivals[part])
            logits(which, part, deltas, first and part == 0)

    for load in loads[2:]:
        load.wait()
    add_boxes(0, own_core, (0,), True)
    pass_on(0)
    start_last(1, ("l1", "r0"))
    for part in parts:
        logits(1, part, (0,), part == 0)
    near = near_to_core(0)
    landed(*near[0])
    logits(0, 0, (3, 1))
    pass_on(1)
    landed(*near[1])
    logits(0, 1, (3, 1))
    far = far_to_core(0)
    landed(*near[2])
    logits(0, 2, (3, 1))
    near1 = near_to_core(1)
    landed(*far[0])
    logits(0, 0, (2,))
    landed(*far[1])
    logits(0, 1, (2,))
    landed(*far[2])
    logits(0, 2, (2,))
    far1 = far_to_core(1)
    near, far = near1, far1
    add_boxes(1, near, (3, 1))
    add_boxes(1, far, (2,))
    for part in parts:
        order = GATHER[part][2]
        sent.append((region(part, order[:2], me, core, wide_axis=order[2]), last_leave[part]))
        sent.append((region(part, AXES, me, core), core_leave[part]))

    lane = lax.broadcasted_iota(jnp.int32, (64, 128), 1)

    def terms(b, carry):
        at = pl.ds(pl.multiple_of(b * 64, 64), 64)
        pairs = [pl.ds(offset_ref[b * 4 + i], 16) for i in range(4)]

        def paired(j):
            return jnp.concatenate([tl[j, pair, :] for pair in pairs], axis=0)

        smax, tmax = sl[0, at, :], paired(0)
        for j in range(1, TILES):
            smax = jnp.maximum(smax, sl[j, at, :])
            tmax = jnp.maximum(tmax, paired(j))
        smax = jnp.max(smax, axis=1, keepdims=True)
        tmax = jnp.max(tmax, axis=1, keepdims=True)
        ssum = tsum = cross = jnp.zeros((64, 128), F32)
        for j in range(TILES):
            s, t = sl[j, at, :], paired(j)
            e = jnp.exp(s - smax)
            sl[j, at, :] = e
            ssum = ssum + e
            e = jnp.exp(t - tmax)
            et[j, at, :] = e
            tsum = tsum + e
            cross = cross + e * (t - s)
        ssum = jnp.sum(ssum, axis=1, keepdims=True)
        tsum = jnp.sum(tsum, axis=1, keepdims=True)
        cross = jnp.sum(cross, axis=1, keepdims=True)
        tile = jnp.where(lane == 0, smax, jnp.where(lane == 1, tmax, jnp.where(lane == 2, ssum, jnp.where(lane == 3, tsum, cross))))
        stat[at, :] = tile
        return carry

    lax.fori_loop(0, 8, terms, 0, unroll=2)

    local = stat[...].T[0:8, :]
    now = local
    slot = 0
    for level in range(2):
        st_send[level] = now
        if level == 0:
            friends = [device(shifted("x", delta), c) for delta in FAR_FIRST for c in (1 - core, core)] + [sibling]
        else:
            friends = [device({**shifted("y", a), "z": shifted("z", b)["z"]}, core) for a, b in PLANE]
        leave, land = fresh(0), fresh(1)
        for i, friend in enumerate(friends):
            post(st_send.at[level], st_recv.at[slot + i], friend, leave, land)
        landing = st_recv.at[pl.ds(slot, len(friends))]
        sent.append((landing, leave))
        landed(landing, land)
        members = [now] + [st_recv[slot + i] for i in range(len(friends))]
        slot += len(friends)
        smax, tmax = members[0][0:1], members[0][1:2]
        for member in members[1:]:
            smax = jnp.maximum(smax, member[0:1])
            tmax = jnp.maximum(tmax, member[1:2])
        ssum = tsum = cross = jnp.zeros((1, 512), F32)
        for member in members:
            a = jnp.exp(member[0:1] - smax)
            b = jnp.exp(member[1:2] - tmax)
            ssum = ssum + member[2:3] * a
            tsum = tsum + member[3:4] * b
            cross = cross + member[4:5] * b
        now = jnp.concatenate([smax, tmax, ssum, tsum, cross, cross, cross, cross], axis=0)
    value = cross / tsum - tmax - jnp.log(tsum) + smax + jnp.log(ssum)
    sscale = jnp.exp(local[0:1] - smax) / ssum
    tscale = jnp.exp(local[1:2] - tmax) / tsum
    filler = jnp.zeros((125, 512), F32)
    stat[...] = jnp.concatenate([sscale, tscale, value, filler], axis=0).T

    row = lax.broadcasted_iota(jnp.int32, (16, 128), 0)
    four = lax.broadcasted_iota(jnp.int32, (4, 128), 0)
    mine = stat[pl.ds(wide * 16 + z * 4, 4), :]
    mine = jnp.where(four + z * 4 < count_ref[wide], jnp.broadcast_to(mine[:, 2:3], (4, 128)), 0.0)
    out_ref[:, 4096:4224] = mine

    def prob_diff(pair, carry):
        for c in range(2):
            g = pair * 2 + c
            half = core if c else 1 - core
            at = pl.ds(pl.multiple_of(g * 16, 16), 16)
            scale = stat[at, :]
            live = row < count_ref[g]
            a = jnp.where(live, jnp.broadcast_to(scale[:, 0:1], (16, 128)), 0.0)
            b = jnp.where(live, jnp.broadcast_to(scale[:, 1:2], (16, 128)), 0.0)
            for j in range(TILES):
                pd[half, pair, :, j * 128:(j + 1) * 128] = (sl[j, at, :] * a - et[j, at, :] * b).astype(BF16)
        return carry

    lax.fori_loop(0, 16, prob_diff, 0, unroll=4)

    core_out, first_out = fresh(0), fresh(0)

    def grad_matmul(j):
        weights = jnp.concatenate([shead[q * 1024 + j * 128:q * 1024 + (j + 1) * 128, :] for q in range(4)], axis=0)
        out = lax.dot_general(
            pd[...].reshape(512, VOCAB), weights, (((1,), (1,)), ((), ())), preferred_element_type=F32
        )
        for q in range(4):
            piece = out[:, q * 128:(q + 1) * 128]
            core_send[j, q] = piece[0:256].astype(BF16).reshape(4, 4, 16, 128)
            own[j, q] = piece[256:512].reshape(4, 4, 16, 128)
    def pick(ref, j, axis, q):
        index = [slice(None)] * 3
        index[AXES.index(axis)] = q
        return ref[(j, *index)]

    boxes = {}

    def first_stage(j, core_land):
        axis = FIRST[j]
        landed(core_recv.at[j], core_land)
        for i, delta in enumerate(FAR_FIRST):
            q = shifted(axis, delta)[axis]
            stage0[j, i] = (pick(own, j, axis, q) + pick(core_recv, j, axis, q).astype(F32)).astype(BF16)

    def first_start(j):
        boxes[j] = fresh(1)
        for i, delta in enumerate(FAR_FIRST):
            post(stage0.at[j, i], recv0.at[j, i], peer(FIRST[j], delta), first_out, boxes[j])

    cur = {"z": curz, "x": curx, "y": cury}
    stage = {"z": stagez, "x": stagex, "y": stagey}
    recv = {"z": recvz, "x": recvx, "y": recvy}

    def first_end(j):
        axis = FIRST[j]
        landed(recv0.at[j], boxes[j])
        total = pick(own, j, axis, me[axis]) + pick(core_recv, j, axis, me[axis]).astype(F32)
        for i in range(3):
            total = total + recv0[j, i].astype(F32)
        place = j - FIRST.index(axis)
        for q in range(4):
            cur[axis][q, place] = total[q] if axis == "z" else total[:, q]

    def second_start(axis):
        leave, land = fresh(0), fresh(1)
        for i, delta in enumerate(FAR_FIRST):
            q = shifted(THEN[axis], delta)[THEN[axis]]
            stage[axis][i] = cur[axis][q].astype(BF16)
            post(stage[axis].at[i], recv[axis].at[i], peer(THEN[axis], delta), leave, land)
        sent.append((stage[axis], leave))
        return land

    def second_end(axis, land):
        landed(recv[axis], land)
        total = cur[axis][me[THEN[axis]]]
        for i in range(3):
            total = total + recv[axis][i].astype(F32)
        return total

    def rows_start(total, fin, got):
        for q in range(4):
            fin[q] = total[:, :, 4 * q:4 * q + 4, :]
        leave, land = fresh(0), fresh(1)
        for delta in FAR_FIRST:
            q = shifted("z", delta)["z"]
            post(fin.at[q], got.at[z], peer("z", delta), leave, land)
        got[z] = fin[z]
        sent.append((fin.at[pl.ds(0, 3)], leave))
        return got.at[pl.ds(0, 3)], land

    core_land = {}
    for n in range(CHUNKS + LAG):
        if n < CHUNKS:
            j = SEQUENCE[n]
            grad_matmul(j)
            core_land[j] = fresh(1)
            post(core_send.at[j], core_recv.at[j], sibling, core_out, core_land[j])
        if n >= LAG:
            first_stage(SEQUENCE[n - LAG], core_land[SEQUENCE[n - LAG]])
            first_start(SEQUENCE[n - LAG])

    sent += [(core_send, core_out), (stage0, first_out)]
    for j in (0, 1):
        first_end(j)
    zland = second_start("z")
    for j in (2, 5, 3, 6, 4):
        first_end(j)
    xland = second_start("x")
    first_end(7)
    yland = second_start("y")
    total = second_end("z", zland)
    for q in range(4):
        curz2[q] = total[:, q]
    leave, land = fresh(0), fresh(1)
    for i, delta in enumerate(FAR_FIRST):
        post(curz2.at[shifted("y", delta)["y"]], recvz2.at[i], peer("y", delta), leave, land)
    sent.append((recvz2, leave))
    xrows = rows_start(second_end("x", xland), finx, gotx)
    yrows = rows_start(second_end("y", yland), finy, goty)
    landed(recvz2, land)
    total = curz2[me["y"]] + recvz2[0] + recvz2[1] + recvz2[2]
    zrows = rows_start(total[None], finz, gotz)
    for axis, arrival, got in (("x", xrows, gotx), ("y", yrows, goty)):
        landed(*arrival)
        total = got[0] + got[1] + got[2] + got[3]
        for place in range(3):
            for q in range(4):
                at = q * 1024 + (FIRST.index(axis) + place) * 128
                out_ref[:, at:at + 128] = total[place, q]
    landed(*zrows)
    for place in range(2):
        for q in range(4):
            at = q * 1024 + place * 128
            out_ref[:, at:at + 128] = gotz[q, 0, place]
    for ref, leave in sent:
        left(ref, leave)
    assert tuple(used) == (SENDS, ARRIVALS), used


def shards(student_hidden, teacher_hidden, student_head, teacher_head, group_counts, group_offsets):
    hbm = pl.BlockSpec(memory_space=pl.ANY)
    head = pltpu.VMEM((4096, VOCAB), BF16)
    table = pltpu.VMEM((TILES, 512, 128), F32)
    scratch = [
        pltpu.VMEM((4, 4096), BF16),
        pltpu.VMEM((4, 4096), BF16),
        pltpu.SMEM((32,), jnp.int32),
        pltpu.SMEM((32,), jnp.int32),
        head, head,
        pltpu.VMEM((2, 4, 4, 4, 2, 16, 1024), BF16),
        table, table, table,
        pltpu.VMEM((2, 16, 16, VOCAB), BF16),
        pltpu.VMEM((4, 16, 512), BF16),
        pltpu.VMEM((4, 16, 512), BF16),
        pltpu.VMEM((4, 16, 512), F32),
        pltpu.VMEM((16, 1024), F32),
        pltpu.VMEM((512, 128), F32),
        pltpu.VMEM((2, 8, 512), F32),
        pltpu.VMEM((22, 8, 512), F32),
        pltpu.VMEM((CHUNKS, 4, 4, 4, 16, 128), BF16),
        pltpu.VMEM((CHUNKS, 4, 4, 4, 16, 128), BF16),
        pltpu.VMEM((CHUNKS, 4, 4, 4, 16, 128), F32),
        pltpu.VMEM((CHUNKS, 3, 4, 4, 16, 128), BF16),
        pltpu.VMEM((CHUNKS, 3, 4, 4, 16, 128), BF16),
        pltpu.VMEM((4, 2, 4, 16, 128), F32),
        pltpu.VMEM((4, 3, 4, 16, 128), F32),
        pltpu.VMEM((4, 3, 4, 16, 128), F32),
        pltpu.VMEM((3, 2, 4, 16, 128), BF16),
        pltpu.VMEM((3, 3, 4, 16, 128), BF16),
        pltpu.VMEM((3, 3, 4, 16, 128), BF16),
        pltpu.VMEM((3, 2, 4, 16, 128), BF16),
        pltpu.VMEM((3, 3, 4, 16, 128), BF16),
        pltpu.VMEM((3, 3, 4, 16, 128), BF16),
        pltpu.VMEM((4, 2, 16, 128), F32),
        pltpu.VMEM((3, 2, 16, 128), F32),
        pltpu.VMEM((4, 1, 2, 4, 128), F32),
        pltpu.VMEM((4, 3, 4, 4, 128), F32),
        pltpu.VMEM((4, 3, 4, 4, 128), F32),
        pltpu.VMEM((4, 1, 2, 4, 128), F32),
        pltpu.VMEM((4, 3, 4, 4, 128), F32),
        pltpu.VMEM((4, 3, 4, 4, 128), F32),
        pltpu.SemaphoreType.DMA((SENDS,)),
        pltpu.SemaphoreType.DMA((ARRIVALS,)),
        pltpu.SemaphoreType.DMA((6,)),
    ]
    out = pl.pallas_call(
        kernel,
        out_shape=jax.ShapeDtypeStruct((4, 4224), F32),
        in_specs=[hbm] * 6,
        out_specs=pl.BlockSpec(memory_space=pltpu.VMEM),
        scratch_shapes=scratch,
        compiler_params=pltpu.CompilerParams(
            collective_id=0, has_side_effects=True, vmem_limit_bytes=60 << 20
        ),
        cost_estimate=pl.CostEstimate(flops=14495514624, bytes_accessed=19000000, transcendentals=1200000),
    )(student_hidden, teacher_hidden, student_head, teacher_head, group_counts, group_offsets)
    return out[:, 4096], out[:, :4096].astype(BF16)


def solution(mesh):
    both = ("wide", "narrow")
    return jax.shard_map(
        shards,
        mesh=mesh,
        in_specs=(P(both, None), P(both, None), P(None, both), P(None, both), P(), P()),
        out_specs=(P(both), P(both, None)),
        check_vma=False,
    )
```

```python
import jax
import jax.numpy as jnp
from jax import lax
from jax.experimental import pallas as pl
from jax.experimental.pallas import tpu as pltpu
from jax.sharding import PartitionSpec as P

MESH = pl.DeviceIdType.MESH
F32, BF16 = jnp.float32, jnp.bfloat16
AXES = ("z", "x", "y")
GATHER = ((0, 256, ("x", "y", "z")), (256, 384, ("y", "z", "x")), (640, 384, ("z", "x", "y")))
FIRST = ("z", "z", "x", "x", "x", "y", "y", "y")
THEN = {"z": "x", "x": "y", "y": "x"}
SEQUENCE = (2, 5, 0, 1, 3, 6, 4, 7)
LAG = 2
PLANE = sorted(((a, b) for a in range(4) for b in range(4) if a or b), key=lambda d: -sum(min(e, 4 - e) for e in d))
CHUNKS = len(FIRST)
SENDS, ARRIVALS = 26, 73
FAR_FIRST = (2, 1, 3)
VOCAB = 1152
TILES = VOCAB // 128


def kernel(
    student_hbm, teacher_hbm, shead_hbm, thead_hbm, count_hbm, offset_hbm,
    out_ref,
    student_ref, teacher_ref, count_ref, offset_ref,
    shead, thead, rows, sl, tl, et, pd,
    pre_send, pre_recv, pack, block, stat, st_send, st_recv,
    core_send, core_recv, own, stage0, recv0,
    curz, curx, cury, stagez, stagex, stagey, recvz, recvx, recvy, curz2, recvz2,
    finz, finx, finy, gotz, gotx, goty,
    send_sem, recv_sem, load_sem,
):
    wide = lax.axis_index("wide")
    me = {"z": lax.axis_index("narrow"), "x": wide // 8, "y": lax.rem(wide // 2, 4)}
    core = lax.rem(wide, 2)

    def device(at, c):
        return ((at["x"] * 4 + at["y"]) * 2 + c, at["z"])

    def shifted(axis, delta):
        return {**me, axis: lax.rem(me[axis] + delta, 4)}

    def peer(axis, delta):
        return device(shifted(axis, delta), core)

    sibling = device(me, 1 - core)
    sent, used = [], [0, 0]

    def fresh(kind):
        used[kind] += 1
        return used[kind] - 1

    def post(src, dst, to, leave, land):
        pltpu.make_async_remote_copy(
            src_ref=src, dst_ref=dst, send_sem=send_sem.at[leave], recv_sem=recv_sem.at[land],
            device_id=to, device_id_type=MESH,
        ).start()

    def landed(ref, land):
        pltpu.make_async_remote_copy(
            src_ref=ref, dst_ref=ref, send_sem=send_sem.at[0], recv_sem=recv_sem.at[land],
            device_id=sibling, device_id_type=MESH,
        ).wait_recv()

    def left(ref, leave):
        pltpu.make_async_remote_copy(
            src_ref=ref, dst_ref=ref, send_sem=send_sem.at[leave], recv_sem=recv_sem.at[0],
            device_id=sibling, device_id_type=MESH,
        ).wait_send()

    loads = [
        pltpu.make_async_copy(src, dst, load_sem.at[i])
        for i, (src, dst) in enumerate((
            (teacher_hbm, teacher_ref), (student_hbm, student_ref), (count_hbm, count_ref),
            (offset_hbm, offset_ref), (thead_hbm, thead), (shead_hbm, shead),
        ))
    ]
    for load in loads:
        load.start()

    barrier = pltpu.get_barrier_semaphore()
    friends = [peer(axis, delta) for axis in AXES for delta in (1, 2, 3)] + [sibling]
    for friend in friends:
        pl.semaphore_signal(barrier, inc=1, device_id=friend, device_id_type=MESH)

    for load in loads[:2]:
        load.wait()
    for q in range(4):
        for h in range(2):
            at = slice(q * 1024 + h * 512, q * 1024 + h * 512 + 512)
            pack[q, 4 * h:4 * h + 4, :] = teacher_ref[:, at].astype(F32)
            pack[q, 8 + 4 * h:12 + 4 * h, :] = student_ref[:, at].astype(F32)
    pre_send[...] = pack[...].astype(BF16)
    pl.semaphore_wait(barrier, len(friends))

    z = me["z"]
    leave, land = fresh(0), fresh(1)
    for delta in FAR_FIRST:
        to = shifted("z", delta)
        post(pre_send.at[to["z"]], pre_recv.at[z], device(to, core), leave, land)
    pre_recv[z] = pre_send[z]
    sent.append((pre_send.at[pl.ds(0, 3)], leave))
    landed(pre_recv.at[pl.ds(0, 3)], land)
    pack[...] = pre_recv[...].astype(F32)
    for which in range(2):
        for s in range(4):
            for h in range(2):
                top = 8 * which + 4 * h
                block[4 * s:4 * s + 4, h * 512:h * 512 + 512] = pack[s, top:top + 4, :]
        rows[which, z, me["x"], me["y"], core] = block[...].astype(BF16)

    def region(part, free, at, c, which=None, half=None, wide_axis=None, count=3):
        start, width, order = GATHER[part]
        index = [pl.ds(0, 2) if which is None else which]
        for axis in AXES:
            if axis == wide_axis:
                index.append(pl.ds(0, count))
            elif axis not in free:
                index.append(at[axis])
            elif half is not None and axis == order[0]:
                index.append(pl.ds(2 * half, 2))
            else:
                index.append(pl.ds(0, 4))
        return rows.at[(*index, c, pl.ds(0, 16), pl.ds(start, width))]

    parts = range(len(GATHER))

    def spread(part, step):
        order = GATHER[part][2]
        here = region(part, order[:step], me, core)
        leave, land = fresh(0), fresh(1)
        for delta in FAR_FIRST:
            post(here, here, peer(order[step], delta), leave, land)
        three = region(part, order[:step], me, core, wide_axis=order[step])
        sent.append((three, leave))
        return three, land

    core_leave = [fresh(0) for _ in parts]
    last_leave = [fresh(0) for _ in parts]
    last_land = [[{name: fresh(1) for name in ("l0", "r1", "near", "far")} for _ in parts] for _ in range(2)]

    def to_core(part, at, land, which=None):
        here = region(part, GATHER[part][2][:2], at, core, which)
        post(here, here, sibling, core_leave[part], land)

    def start_last(which, names):
        for part in parts:
            order = GATHER[part][2]
            for name in names:
                here = region(part, order[:2], me, core, which, int(name[1]))
                land = last_land[which][part][name if name in ("l0", "r1") else "near"]
                post(here, here, peer(order[2], 1 if name[0] == "l" else 3), last_leave[part], land)

    def pass_on(which):
        for part in parts:
            order = GATHER[part][2]
            for name, delta, half, to in (("l0", 3, 0, 1), ("r1", 1, 1, 3)):
                here = region(part, order[:2], shifted(order[2], delta), core, which, half)
                landed(here, last_land[which][part][name])
                post(here, here, peer(order[2], to), last_leave[part], last_land[which][part]["far"])

    def box_to_core(which, name, deltas):
        arrivals = []
        for part in parts:
            axis, free = GATHER[part][2][2], GATHER[part][2][:2]
            landed(region(part, free, me, core, which), last_land[which][part][name])
            land = fresh(1)
            for delta in deltas:
                to_core(part, shifted(axis, delta), land, which)
            arrivals.append((region(part, free, me, core, which, wide_axis=axis, count=len(deltas)), land))
        return arrivals

    def near_to_core(which):
        return box_to_core(which, "near", (3, 1))

    def far_to_core(which):
        return box_to_core(which, "far", (2,))

    step0 = [spread(part, 0) for part in parts]
    step1 = []
    for part in parts:
        landed(*step0[part])
        step1.append(spread(part, 1))
    for part in parts:
        landed(*step1[part])
    start_last(0, ("l0", "r1", "l1", "r0"))
    own_core = []
    for part in parts:
        land = fresh(1)
        to_core(part, me, land)
        own_core.append((region(part, GATHER[part][2][:2], me, core), land))

    start_last(1, ("l0", "r1"))
    def logits(which, part, deltas, first=False):
        start, width, order = GATHER[part]
        axis = order[2]
        head, out = ((thead, tl), (shead, sl))[which]
        places = [shifted(axis, delta)[axis] for delta in deltas]
        cols = slice(start, start + width)
        if axis == "z":
            lhs = jnp.concatenate([rows[which, q, :, :, :, :, cols].reshape(512, width) for q in places], axis=1)
            tops = [pl.multiple_of(q * 1024 + start, 128) for q in places]
        else:
            lhs = jnp.concatenate([
                jnp.concatenate([
                    (rows[which, q, v, :, :, :, cols] if axis == "x" else rows[which, q, :, v, :, :, cols]).reshape(128, width)
                    for q in range(4)
                ], axis=1)
                for v in places
            ], axis=0)
            tops = [q * 1024 + start for q in range(4)]
        for tile in range(0, TILES, 2):
            count = min(2, TILES - tile)
            rhs = jnp.concatenate([head[pl.ds(top, width), tile * 128:(tile + count) * 128] for top in tops], axis=0)
            total = jnp.dot(lhs, rhs, preferred_element_type=F32)
            for i in range(count):
                piece = total[:, i * 128:(i + 1) * 128]
                if first:
                    out[tile + i] = piece
                elif axis == "z":
                    out[tile + i] += piece
                else:
                    for n, v in enumerate(places):
                        if axis == "x":
                            at = pl.ds(pl.multiple_of(v * 128, 128), 128)
                            out[tile + i, at, :] += piece[n * 128:(n + 1) * 128]
                        else:
                            for x in range(4):
                                at = pl.ds(pl.multiple_of(x * 128 + v * 32, 32), 32)
                                out[tile + i, at, :] += piece[n * 128 + x * 32:n * 128 + x * 32 + 32]

    def add_boxes(which, arrivals, deltas, first=False):
        for part in parts:
            landed(*arrivals[part])
            logits(which, part, deltas, first and part == 0)

    for load in loads[2:]:
        load.wait()
    add_boxes(0, own_core, (0,), True)
    pass_on(0)
    start_last(1, ("l1", "r0"))
    for part in parts:
        logits(1, part, (0,), part == 0)
    near = near_to_core(0)
    landed(*near[0])
    logits(0, 0, (3, 1))
    pass_on(1)
    landed(*near[1])
    logits(0, 1, (3, 1))
    far = far_to_core(0)
    landed(*near[2])
    logits(0, 2, (3, 1))
    near1 = near_to_core(1)
    landed(*far[0])
    logits(0, 0, (2,))
    landed(*far[1])
    logits(0, 1, (2,))
    landed(*far[2])
    logits(0, 2, (2,))
    far1 = far_to_core(1)
    near, far = near1, far1
    add_boxes(1, near, (3, 1))
    add_boxes(1, far, (2,))
    for part in parts:
        order = GATHER[part][2]
        sent.append((region(part, order[:2], me, core, wide_axis=order[2]), last_leave[part]))
        sent.append((region(part, AXES, me, core), core_leave[part]))

    lane = lax.broadcasted_iota(jnp.int32, (64, 128), 1)

    def terms(b, carry):
        at = pl.ds(pl.multiple_of(b * 64, 64), 64)
        pairs = [pl.ds(offset_ref[b * 4 + i], 16) for i in range(4)]

        def paired(j):
            return jnp.concatenate([tl[j, pair, :] for pair in pairs], axis=0)

        smax, tmax = sl[0, at, :], paired(0)
        for j in range(1, TILES):
            smax = jnp.maximum(smax, sl[j, at, :])
            tmax = jnp.maximum(tmax, paired(j))
        smax = jnp.max(smax, axis=1, keepdims=True)
        tmax = jnp.max(tmax, axis=1, keepdims=True)
        ssum = tsum = cross = jnp.zeros((64, 128), F32)
        for j in range(TILES):
            s, t = sl[j, at, :], paired(j)
            e = jnp.exp(s - smax)
            sl[j, at, :] = e
            ssum = ssum + e
            e = jnp.exp(t - tmax)
            et[j, at, :] = e
            tsum = tsum + e
            cross = cross + e * (t - s)
        ssum = jnp.sum(ssum, axis=1, keepdims=True)
        tsum = jnp.sum(tsum, axis=1, keepdims=True)
        cross = jnp.sum(cross, axis=1, keepdims=True)
        tile = jnp.where(lane == 0, smax, jnp.where(lane == 1, tmax, jnp.where(lane == 2, ssum, jnp.where(lane == 3, tsum, cross))))
        stat[at, :] = tile
        return carry

    lax.fori_loop(0, 8, terms, 0, unroll=2)

    local = stat[...].T[0:8, :]
    now = local
    slot = 0
    for level in range(2):
        st_send[level] = now
        if level == 0:
            friends = [device(shifted("x", delta), c) for delta in FAR_FIRST for c in (1 - core, core)] + [sibling]
        else:
            friends = [device({**shifted("y", a), "z": shifted("z", b)["z"]}, core) for a, b in PLANE]
        leave, land = fresh(0), fresh(1)
        for i, friend in enumerate(friends):
            post(st_send.at[level], st_recv.at[slot + i], friend, leave, land)
        landing = st_recv.at[pl.ds(slot, len(friends))]
        sent.append((landing, leave))
        landed(landing, land)
        members = [now] + [st_recv[slot + i] for i in range(len(friends))]
        slot += len(friends)
        smax, tmax = members[0][0:1], members[0][1:2]
        for member in members[1:]:
            smax = jnp.maximum(smax, member[0:1])
            tmax = jnp.maximum(tmax, member[1:2])
        ssum = tsum = cross = jnp.zeros((1, 512), F32)
        for member in members:
            a = jnp.exp(member[0:1] - smax)
            b = jnp.exp(member[1:2] - tmax)
            ssum = ssum + member[2:3] * a
            tsum = tsum + member[3:4] * b
            cross = cross + member[4:5] * b
        now = jnp.concatenate([smax, tmax, ssum, tsum, cross, cross, cross, cross], axis=0)
    value = cross / tsum - tmax - jnp.log(tsum) + smax + jnp.log(ssum)
    sscale = jnp.exp(local[0:1] - smax) / ssum
    tscale = jnp.exp(local[1:2] - tmax) / tsum
    filler = jnp.zeros((125, 512), F32)
    stat[...] = jnp.concatenate([sscale, tscale, value, filler], axis=0).T

    row = lax.broadcasted_iota(jnp.int32, (16, 128), 0)
    four = lax.broadcasted_iota(jnp.int32, (4, 128), 0)
    mine = stat[pl.ds(wide * 16 + z * 4, 4), :]
    mine = jnp.where(four + z * 4 < count_ref[wide], jnp.broadcast_to(mine[:, 2:3], (4, 128)), 0.0)
    out_ref[:, 4096:4224] = mine

    def prob_diff(pair, carry):
        for c in range(2):
            g = pair * 2 + c
            half = core if c else 1 - core
            at = pl.ds(pl.multiple_of(g * 16, 16), 16)
            scale = stat[at, :]
            live = row < count_ref[g]
            a = jnp.where(live, jnp.broadcast_to(scale[:, 0:1], (16, 128)), 0.0)
            b = jnp.where(live, jnp.broadcast_to(scale[:, 1:2], (16, 128)), 0.0)
            for j in range(TILES):
                pd[half, pair, :, j * 128:(j + 1) * 128] = (sl[j, at, :] * a - et[j, at, :] * b).astype(BF16)
        return carry

    lax.fori_loop(0, 16, prob_diff, 0, unroll=4)

    core_out, first_out = fresh(0), fresh(0)

    def grad_matmul(j):
        weights = jnp.concatenate([shead[q * 1024 + j * 128:q * 1024 + (j + 1) * 128, :] for q in range(4)], axis=0)
        out = lax.dot_general(
            pd[...].reshape(512, VOCAB), weights, (((1,), (1,)), ((), ())), preferred_element_type=F32
        )
        for q in range(4):
            piece = out[:, q * 128:(q + 1) * 128]
            core_send[j, q] = piece[0:256].astype(BF16).reshape(4, 4, 16, 128)
            own[j, q] = piece[256:512].reshape(4, 4, 16, 128)
    def pick(ref, j, axis, q):
        index = [slice(None)] * 3
        index[AXES.index(axis)] = q
        return ref[(j, *index)]

    boxes = {}

    def first_stage(j, core_land):
        axis = FIRST[j]
        landed(core_recv.at[j], core_land)
        for i, delta in enumerate(FAR_FIRST):
            q = shifted(axis, delta)[axis]
            stage0[j, i] = (pick(own, j, axis, q) + pick(core_recv, j, axis, q).astype(F32)).astype(BF16)

    def first_start(j):
        boxes[j] = fresh(1)
        for i, delta in enumerate(FAR_FIRST):
            post(stage0.at[j, i], recv0.at[j, i], peer(FIRST[j], delta), first_out, boxes[j])

    cur = {"z": curz, "x": curx, "y": cury}
    stage = {"z": stagez, "x": stagex, "y": stagey}
    recv = {"z": recvz, "x": recvx, "y": recvy}

    def first_end(j):
        axis = FIRST[j]
        landed(recv0.at[j], boxes[j])
        total = pick(own, j, axis, me[axis]) + pick(core_recv, j, axis, me[axis]).astype(F32)
        for i in range(3):
            total = total + recv0[j, i].astype(F32)
        place = j - FIRST.index(axis)
        for q in range(4):
            cur[axis][q, place] = total[q] if axis == "z" else total[:, q]

    def second_start(axis, low, count):
        leave, land = fresh(0), fresh(1)
        tiles = pl.ds(low, count)
        for i, delta in enumerate(FAR_FIRST):
            q = shifted(THEN[axis], delta)[THEN[axis]]
            stage[axis][i, tiles] = cur[axis][q, tiles].astype(BF16)
            post(stage[axis].at[i, tiles], recv[axis].at[i, tiles], peer(THEN[axis], delta), leave, land)
        sent.append((stage[axis].at[pl.ds(0, 3), tiles], leave))
        return recv[axis].at[pl.ds(0, 3), tiles], land

    def second_end(axis, arrivals):
        for arrival in arrivals:
            landed(*arrival)
        total = cur[axis][me[THEN[axis]]]
        for i in range(3):
            total = total + recv[axis][i].astype(F32)
        return total

    def rows_start(total, fin, got):
        for q in range(4):
            fin[q] = total[:, :, 4 * q:4 * q + 4, :]
        leave, land = fresh(0), fresh(1)
        for delta in FAR_FIRST:
            q = shifted("z", delta)["z"]
            post(fin.at[q], got.at[z], peer("z", delta), leave, land)
        got[z] = fin[z]
        sent.append((fin.at[pl.ds(0, 3)], leave))
        return got.at[pl.ds(0, 3)], land

    core_land = {}
    for n in range(CHUNKS + LAG):
        if n < CHUNKS:
            j = SEQUENCE[n]
            grad_matmul(j)
            core_land[j] = fresh(1)
            post(core_send.at[j], core_recv.at[j], sibling, core_out, core_land[j])
        if n >= LAG:
            first_stage(SEQUENCE[n - LAG], core_land[SEQUENCE[n - LAG]])
            first_start(SEQUENCE[n - LAG])

    sent += [(core_send, core_out), (stage0, first_out)]
    for j in (0, 1):
        first_end(j)
    zland = [second_start("z", 0, 2)]
    for j in (2, 3):
        first_end(j)
    xland = [second_start("x", 0, 2)]
    for j in (5, 6):
        first_end(j)
    yland = [second_start("y", 0, 2)]
    first_end(4)
    xland.append(second_start("x", 2, 1))
    first_end(7)
    yland.append(second_start("y", 2, 1))
    total = second_end("z", zland)
    for q in range(4):
        curz2[q] = total[:, q]
    leave, land = fresh(0), fresh(1)
    for i, delta in enumerate(FAR_FIRST):
        post(curz2.at[shifted("y", delta)["y"]], recvz2.at[i], peer("y", delta), leave, land)
    sent.append((recvz2, leave))
    xrows = rows_start(second_end("x", xland), finx, gotx)
    yrows = rows_start(second_end("y", yland), finy, goty)
    landed(recvz2, land)
    total = curz2[me["y"]] + recvz2[0] + recvz2[1] + recvz2[2]
    zrows = rows_start(total[None], finz, gotz)
    for axis, arrival, got in (("x", xrows, gotx), ("y", yrows, goty)):
        landed(*arrival)
        total = got[0] + got[1] + got[2] + got[3]
        for place in range(3):
            for q in range(4):
                at = q * 1024 + (FIRST.index(axis) + place) * 128
                out_ref[:, at:at + 128] = total[place, q]
    landed(*zrows)
    for place in range(2):
        for q in range(4):
            at = q * 1024 + place * 128
            out_ref[:, at:at + 128] = gotz[q, 0, place]
    for ref, leave in sent:
        left(ref, leave)
    assert tuple(used) == (SENDS, ARRIVALS), used


def shards(student_hidden, teacher_hidden, student_head, teacher_head, group_counts, group_offsets):
    hbm = pl.BlockSpec(memory_space=pl.ANY)
    head = pltpu.VMEM((4096, VOCAB), BF16)
    table = pltpu.VMEM((TILES, 512, 128), F32)
    scratch = [
        pltpu.VMEM((4, 4096), BF16),
        pltpu.VMEM((4, 4096), BF16),
        pltpu.SMEM((32,), jnp.int32),
        pltpu.SMEM((32,), jnp.int32),
        head, head,
        pltpu.VMEM((2, 4, 4, 4, 2, 16, 1024), BF16),
        table, table, table,
        pltpu.VMEM((2, 16, 16, VOCAB), BF16),
        pltpu.VMEM((4, 16, 512), BF16),
        pltpu.VMEM((4, 16, 512), BF16),
        pltpu.VMEM((4, 16, 512), F32),
        pltpu.VMEM((16, 1024), F32),
        pltpu.VMEM((512, 128), F32),
        pltpu.VMEM((2, 8, 512), F32),
        pltpu.VMEM((22, 8, 512), F32),
        pltpu.VMEM((CHUNKS, 4, 4, 4, 16, 128), BF16),
        pltpu.VMEM((CHUNKS, 4, 4, 4, 16, 128), BF16),
        pltpu.VMEM((CHUNKS, 4, 4, 4, 16, 128), F32),
        pltpu.VMEM((CHUNKS, 3, 4, 4, 16, 128), BF16),
        pltpu.VMEM((CHUNKS, 3, 4, 4, 16, 128), BF16),
        pltpu.VMEM((4, 2, 4, 16, 128), F32),
        pltpu.VMEM((4, 3, 4, 16, 128), F32),
        pltpu.VMEM((4, 3, 4, 16, 128), F32),
        pltpu.VMEM((3, 2, 4, 16, 128), BF16),
        pltpu.VMEM((3, 3, 4, 16, 128), BF16),
        pltpu.VMEM((3, 3, 4, 16, 128), BF16),
        pltpu.VMEM((3, 2, 4, 16, 128), BF16),
        pltpu.VMEM((3, 3, 4, 16, 128), BF16),
        pltpu.VMEM((3, 3, 4, 16, 128), BF16),
        pltpu.VMEM((4, 2, 16, 128), F32),
        pltpu.VMEM((3, 2, 16, 128), F32),
        pltpu.VMEM((4, 1, 2, 4, 128), F32),
        pltpu.VMEM((4, 3, 4, 4, 128), F32),
        pltpu.VMEM((4, 3, 4, 4, 128), F32),
        pltpu.VMEM((4, 1, 2, 4, 128), F32),
        pltpu.VMEM((4, 3, 4, 4, 128), F32),
        pltpu.VMEM((4, 3, 4, 4, 128), F32),
        pltpu.SemaphoreType.DMA((SENDS,)),
        pltpu.SemaphoreType.DMA((ARRIVALS,)),
        pltpu.SemaphoreType.DMA((6,)),
    ]
    out = pl.pallas_call(
        kernel,
        out_shape=jax.ShapeDtypeStruct((4, 4224), F32),
        in_specs=[hbm] * 6,
        out_specs=pl.BlockSpec(memory_space=pltpu.VMEM),
        scratch_shapes=scratch,
        compiler_params=pltpu.CompilerParams(
            collective_id=0, has_side_effects=True, vmem_limit_bytes=60 << 20
        ),
        cost_estimate=pl.CostEstimate(flops=14495514624, bytes_accessed=19000000, transcendentals=1200000),
    )(student_hidden, teacher_hidden, student_head, teacher_head, group_counts, group_offsets)
    return out[:, 4096], out[:, :4096].astype(BF16)


def solution(mesh):
    both = ("wide", "narrow")
    return jax.shard_map(
        shards,
        mesh=mesh,
        in_specs=(P(both, None), P(both, None), P(None, both), P(None, both), P(), P()),
        out_specs=(P(both), P(both, None)),
        check_vma=False,
    )
```
